128 devices in a mesh: comp: 4 (over x_hi, core), tile: 32 (over x_lo, z, y).
Axes of the slice: x: 4 (x_hi: 2, x_lo: 2; x = x_hi * 2 + x_lo), y: 4, z: 4, core: 2. Of those that a mesh axis runs over, the one named last changes fastest.
Arguments:
- state: float32 [60, 128, 24576], P(None, 'comp', 'tile'), may hold values from -6 to 6
- kappa: float32 [128, 24576], P('comp', 'tile'), may hold values from 0.03 to 0.24
- land_mask: int32 [128, 24576], P('comp', 'tile'), may hold values 0 or 1
- remap_weight: bfloat16 [16384, 128, 128], P(('comp', 'tile')), may hold values from -0.5 to 0.5
- remap_src: int32 [16384], P(('comp', 'tile')), may hold values from 0 to 191
- remap_tile: int32 [16384, 1], P(('comp', 'tile')), may hold values from 0 to 31; in each aligned block of 128 rows (0 to 127, 128 to 255, ...) at most 6 rows name the same one
- remap_block: int32 [16384], P(('comp', 'tile')), may hold values from 0 to 575
- remap_count: int32 [128], P(('comp', 'tile')), may hold values from 64 to 128, as said below
Outputs:
- state_next: float32 [60, 128, 24576], P(None, 'comp', 'tile')
The draws below stay inside these ranges and needn't reach their ends.
Inputs may be any that keep to these rules, and one draw needn't show every extreme that they name: `remap_tile`: each device's 128 entries name no tile more than 6 times. `remap_count`: some device has all 128 blocks live.
All inputs are finite; a program needn't handle non-finite values. No bound on the sum of `land_mask` on one device may be relied on, other than what follows from the above.
Results may differ from the reference program's by a relative error of at most 0.0003.
Values sent between devices are 32-bit elements; how exact they have to be, the bound alone decides.
A program may use at most 128 MiB of HBM per device.

```python
import math
import jax
import jax.numpy as jnp
import numpy as np
from jax import lax

COUPLED = 3
BLK = 128
SUB = 4
BY = 32
BX = 768
NBD = 128
ROWS = 60
NDEV = 128
NBLK = 192
CAP = 6
NY = 128
NX = 24576
N_COMP = 4
N_TILE = 32


def draw_remap_count(key, part):
    key = jax.random.fold_in(key, 7)
    draw_key, pick_key = jax.random.split(key)
    counts = jax.random.randint(draw_key, (NDEV,), NBD // 2, NBD + 1)
    fullest = jax.random.randint(pick_key, (), 0, NDEV)
    return jnp.where(jnp.arange(NDEV) == fullest, NBD, counts).astype(jnp.int32)


def touch_ends(drawn, rng, smallest, largest):
    shape = drawn.shape
    place = [jax.random.randint(jax.random.fold_in(rng, axis), (), 0, shape[axis]) for axis in range(len(shape))]
    drawn = drawn.at[tuple(place)].set(smallest)
    longest = shape.index(max(shape))
    place[longest] = (place[longest] + 1) % shape[longest]
    return drawn.at[tuple(place)].set(largest)


def shard_levels(own_key, shape, pieces, low, high):
    loudness = 1.0
    for axis_at, blocks in pieces:
        heights = jax.random.uniform(jax.random.fold_in(jax.random.fold_in(own_key, 6), axis_at), (blocks,), jnp.float32, low / len(pieces), high / len(pieces))
        loudness = loudness * jnp.repeat(jnp.exp(heights), shape[axis_at] // blocks).reshape((-1,) + (1,) * (len(shape) - 1 - axis_at))
    return loudness


def routed_block(stream_key, own, number, rows, amount, top, limit, lean):
    sequence = jax.random.permutation(stream_key, amount)
    heavy_load, ordinary = shares(amount, rows * top, limit, lean, True), shares(amount, rows * top, limit, lean, False)
    places = jnp.arange(amount)

    def named(lengths, turn):
        used = int((lengths > 0).sum())
        fixed = max(1, used // 4)
        passed = fixed + (places - fixed + turn * (used - fixed)) % max(1, amount - fixed)
        return jnp.zeros((amount,), jnp.int32).at[sequence[jnp.where(places < fixed, places, passed)]].set(jnp.asarray(lengths, jnp.int32))

    lengths = jnp.where(number % 4 == 0, named(heavy_load, number // 4), named(ordinary, number - number // 4 - 1))
    mixed = jax.random.permutation(jax.random.fold_in(own, 3), amount)
    donor, taker = mixed[0:amount // 2 * 2:2], mixed[1:amount // 2 * 2:2]
    slack = jnp.minimum(lengths[donor] - 1, limit - lengths[taker]) // 2
    slack = jnp.where((donor == sequence[0]) | (taker == sequence[0]) | (lengths[taker] == 0), 0, jnp.maximum(slack, 0))
    passed = jax.random.randint(jax.random.fold_in(own, 4), (amount // 2,), 0, 1 << 20) % (slack + 1)
    lengths = lengths.at[donor].add(-passed).at[taker].add(passed)
    items = jnp.searchsorted(jnp.cumsum(lengths), jnp.arange(rows * top), side="right").astype(jnp.int32)
    table = items.reshape(top, rows).T
    table = table[jax.random.permutation(jax.random.fold_in(own, 1), rows)]
    turn = jax.random.randint(jax.random.fold_in(own, 2), (rows, 1), 0, top)
    return jnp.take_along_axis(table, (jnp.arange(top)[None, :] + turn) % top, axis=1)


def shares(number_of, total, limit, slope, full):
    loads = [(1 << 20) // math.isqrt(grade ** slope) + 1 for grade in range(1, number_of + 1)]
    largest = limit if full else min(limit, max(-(-total // number_of), total * loads[0] // sum(loads)))
    least = 1 if total - largest >= number_of - 1 else 0
    given, surplus = [largest] + [least] * (number_of - 1), total - largest - least * (number_of - 1)
    while surplus > 0:
        movable = [i for i in range(1, number_of) if given[i] < largest] or [i for i in range(1, number_of) if given[i] < limit]
        pool, budget = sum([loads[i] for i in movable]), surplus
        for i in movable:
            addition = min(limit - given[i], max(1, budget * loads[i] // pool), surplus)
            given[i] = given[i] + addition
            surplus = surplus - addition
    return np.array(given)


def centred(stream_key, dims, width, most, shards=(), held_as=jnp.bfloat16):
    values = jax.random.normal(stream_key, dims, jnp.float32) * width
    if len(shards) > 0:
        values = shard_levels(stream_key, dims, shards, -0.22, 0.18) * values
    return jnp.clip(values, min=-most, max=most).astype(held_as)


def setup_inputs(seed: int = 0) -> dict:
    key_list = jax.random.split(jax.random.key(seed), 9)
    state = centred(key_list[0], (ROWS, NY, NX), 1.0, 6.0, ((1, 4), (2, 32)), jnp.float32)
    kappa = jnp.clip(jnp.exp(math.log(0.24) - 2.0794415 * jax.random.uniform(key_list[1], (NY, NX), jnp.float32) ** shard_levels(key_list[1], (NY, NX), ((0, 4), (1, 32)), -0.2, 0.2)), 0.03, 0.24)
    land_mask = touch_ends((jax.random.randint(key_list[2], (NY, NX), 0, 4) < 3).astype(jnp.int32), jax.random.fold_in(key_list[2], 1), 0, 1)
    remap_weight = centred(key_list[3], (NDEV * NBD, BLK, BLK), BLK ** -0.5, 0.5, ((0, 128),))
    remap_src = touch_ends(jax.random.randint(key_list[4], (NDEV * NBD,), 0, NBLK), jax.random.fold_in(key_list[4], 1), 0, NBLK - 1).astype(jnp.int32)
    remap_tile_keys = jax.random.split(jax.random.fold_in(key_list[5], 1), (NDEV * NBD) // NBD)
    remap_tile_turns = jax.random.permutation(jax.random.fold_in(key_list[5], 3), (NDEV * NBD) // NBD)
    remap_tile = jax.vmap(lambda own, number: routed_block(jax.random.fold_in(key_list[5], 2), own, number, NBD, N_TILE, 1, CAP, 2))(remap_tile_keys, remap_tile_turns).reshape((NDEV * NBD, 1))
    remap_block = touch_ends(jax.random.randint(key_list[6], (NDEV * NBD,), 0, (N_COMP - 1) * NBLK), jax.random.fold_in(key_list[6], 1), 0, ((N_COMP - 1) * NBLK) - 1).astype(jnp.int32)
    remap_count = draw_remap_count(jax.random.fold_in(key_list[8], 71), 0)
    return dict(state=state, kappa=kappa, land_mask=land_mask, remap_weight=remap_weight, remap_src=remap_src, remap_tile=remap_tile, remap_block=remap_block, remap_count=remap_count)


def band_factors(mask_field, atmos_rows, total_rows):
    global_rows = jnp.arange(total_rows, dtype=jnp.int32)
    following = global_rows + 1
    joined = (following < total_rows) & ((global_rows < atmos_rows) == (following < atmos_rows))
    ocean_rows = (global_rows >= atmos_rows)[:, None]
    mask_above = jnp.roll(mask_field, -1, axis=0)
    mask_right = jnp.roll(mask_field, -1, axis=1)
    open_up = jnp.where(ocean_rows, mask_field * mask_above, 1.0) * joined[:, None].astype(jnp.float32)
    open_right = jnp.where(ocean_rows, mask_field * mask_right, 1.0)
    return open_up, open_right


def diffuse(field, diffusivity, open_up, open_right):
    right_cells = jnp.roll(field, -1, axis=2)
    left_cells = jnp.roll(field, 1, axis=2)
    upper_cells = jnp.roll(field, -1, axis=1)
    lower_cells = jnp.roll(field, 1, axis=1)
    open_left = jnp.roll(open_right, 1, axis=1)
    open_down = jnp.roll(open_up, 1, axis=0)
    laplace = (open_right * (right_cells - field) - open_left * (field - left_cells)
               + open_up * (upper_cells - field) - open_down * (field - lower_cells))
    return field + diffusivity * laplace


def remap_device(pair):
    picked, weights = pair
    return jnp.einsum('kfi,kij->kfj', picked.astype(jnp.float32), weights.astype(jnp.float32))


def reference(state, kappa, land_mask, remap_weight, remap_src, remap_tile, remap_block, remap_count):
    comp_count = N_COMP
    tile_count = N_TILE
    total_rows = comp_count * BY
    atmos_rows = (comp_count - 1) * BY
    block_cols = BX // BLK
    block_count = BY * BX // BLK
    surface = state[:COUPLED].astype(jnp.bfloat16)
    surface = surface.reshape(COUPLED, comp_count, BY, tile_count, block_cols, BLK)
    surface = surface.transpose(1, 3, 2, 4, 0, 5).reshape(NDEV, block_count, COUPLED, BLK)
    slot_device = jnp.arange(NDEV * NBD, dtype=jnp.int32) // NBD
    picked = surface[slot_device, remap_src]
    contributions = lax.map(remap_device, (picked.reshape(NDEV, NBD, COUPLED, BLK), remap_weight.reshape(NDEV, NBD, BLK, BLK)))
    contributions = contributions.reshape(NDEV * NBD, COUPLED, BLK)
    active = (jnp.arange(NDEV * NBD, dtype=jnp.int32) % NBD) < remap_count[slot_device]
    on_ocean = slot_device // tile_count == comp_count - 1
    dest_comp = jnp.where(on_ocean, remap_block // block_count, comp_count - 1)
    target = (dest_comp * tile_count + remap_tile[:, 0]) * block_count + remap_block % block_count
    target = jnp.where(active, target, NDEV * block_count).astype(jnp.int32)
    received = jnp.zeros((NDEV * block_count, COUPLED, BLK), jnp.float32).at[target].add(contributions, mode="drop")
    received = received.reshape(comp_count, tile_count, BY, block_cols, COUPLED, BLK)
    received = received.transpose(4, 0, 2, 1, 3, 5).reshape(COUPLED, total_rows, tile_count * BX)
    mask_field = land_mask.astype(jnp.float32)
    coupled = state[:COUPLED] + 0.5 * mask_field * (received - state[:COUPLED])
    field = jnp.concatenate([coupled, state[COUPLED:]], axis=0)
    open_up, open_right = band_factors(mask_field, atmos_rows, total_rows)
    for substep in range(SUB):
        field = diffuse(field, kappa, open_up, open_right)
    return field
```

```python
import functools

import jax
import jax.numpy as jnp
from jax import lax
from jax.experimental import pallas as pl
from jax.experimental.pallas import tpu as pltpu
from jax.sharding import PartitionSpec as P

LEVELS = 60
COUPLED = 3
BLK = 128
SUB = 4
BY = 32
BX = 768
WIDE = 896
HALO = 4
SLOTS = 128
CAP = 6
TILES = 32
COMPS = 4
OCEAN = COMPS - 1
BLOCKS = 192
COLS = BX // BLK
KAPPA = 60
MASK = 61
HELD = 64
PAIR = 7
CHUNKS = ((3, 22), (22, 41), (41, 61))
WEIGHT_CHUNKS = 4
FIRST = 40
GROUP = min(16, TILES)
MESH = pl.DeviceIdType.MESH
F32 = jnp.float32
BF16 = jnp.bfloat16


def iota(shape, axis):
    return lax.broadcasted_iota(jnp.int32, shape, axis)


def split(x):
    high = x.astype(BF16)
    return high, (x - high.astype(F32)).astype(BF16)


def dot(a, b):
    return jnp.dot(a, b, preferred_element_type=F32)


def to_column(row):
    eye = iota((BLK, BLK), 0) == iota((BLK, BLK), 1)
    return jnp.sum(jnp.where(eye, row, 0.0), axis=1, keepdims=True)


def to_row(column):
    eye = iota((BLK, BLK), 0) == iota((BLK, BLK), 1)
    return jnp.sum(jnp.where(eye, column, 0.0), axis=0, keepdims=True)


def block_place(block):
    row = jnp.floor((block + 0.5) * (1.0 / COLS))
    return (block - COLS * row) * BY + row


def edge_tile(first, second, i):
    a = pltpu.roll(first, lax.rem(BLK - HALO * i, BLK), 1)
    b = pltpu.roll(second, BLK - HALO - HALO * i, 1)
    return jnp.where(iota(a.shape, 1) < BLK // 2, a, b)


def atmos_steps(v, coef):
    for step in range(SUB):
        centre = coef[0][...]
        around = coef[1][...]
        near = (
            pltpu.roll(v, 1, 1)
            + pltpu.roll(v, WIDE - 1, 1)
            + pltpu.roll(v, 1, 0)
            + pltpu.roll(v, BY + 2 * HALO - 1, 0)
        )
        v = centre * v + around * near
    return v[:BY, :BX]


def ocean_steps(v, coef):
    for step in range(SUB):
        v = (
            coef[0][:BY] * v
            + coef[1][:BY] * pltpu.roll(v, WIDE - 1, 1)
            + coef[2][:BY] * pltpu.roll(v, 1, 1)
            + coef[3][:BY] * pltpu.roll(v, BY - 1, 0)
            + coef[4][:BY] * pltpu.roll(v, 1, 0)
        )
    return v[:, :BX]


def level_steps(ocean, field, rows, first, second, coef, level, i):
    edge = edge_tile(first, second, i)
    own = field[level]
    if ocean:
        return ocean_steps(jnp.concatenate([own, edge[:BY]], axis=1), coef)
    tall = jnp.concatenate([own, rows[level]], axis=0)
    return atmos_steps(jnp.concatenate([tall, edge], axis=1), coef)


def diffuse_levels(ocean, field, rows, sides, coef, start, stop, out, shift=0):
    for group in range(2):
        low, high = max(start, group * 32), min(stop, group * 32 + 32)
        if low >= high:
            continue

        def one(level, carry, group=group):
            out[level - shift] = level_steps(
                ocean, field, rows, sides[0, group], sides[1, group], coef, level, level - group * 32
            )
            return carry

        lax.fori_loop(low, high, one, 0)


def exchange_kernel(
    state, kappa, mask, weight, src, tile_of, block_of, count,
    field, rows, late_sides, coef,
    sides, weights, mask_in, send, received, contrib, pack, late_pack,
    load_sem, weight_sem, state_sem, remap_send, remap_recv, row_send, row_recv, side_sem, late_sem,
):
    comp = lax.axis_index("comp")
    tile = lax.axis_index("tile")
    right = lax.rem(tile + 1, TILES)
    left = lax.rem(tile + TILES - 1, TILES)
    is_ocean = comp == OCEAN
    has_up = comp < OCEAN - 1
    has_down = (comp > 0) & (comp < OCEAN)

    load_surface = pltpu.make_async_copy(state.at[pl.ds(0, COUPLED)], field.at[pl.ds(0, COUPLED)], load_sem.at[0])
    load_surface.start()
    load_mask = pltpu.make_async_copy(mask, mask_in, load_sem.at[1])
    load_mask.start()
    load_kappa = pltpu.make_async_copy(kappa, field.at[KAPPA], load_sem.at[2])
    load_kappa.start()
    per = SLOTS // WEIGHT_CHUNKS
    load_weights = [
        pltpu.make_async_copy(weight.at[pl.ds(n * per, per)], weights.at[pl.ds(n * per, per)], weight_sem.at[n])
        for n in range(WEIGHT_CHUNKS)
    ]
    for copy in load_weights:
        copy.start()
    load_state = pltpu.make_async_copy(
        state.at[pl.ds(COUPLED, LEVELS - COUPLED)], field.at[pl.ds(COUPLED, LEVELS - COUPLED)], state_sem
    )
    load_state.start()

    barrier = pltpu.get_barrier_semaphore()

    def greet(c, t):
        pl.semaphore_signal(barrier, inc=1, device_id=(c, t), device_id_type=MESH)

    received[:, PAIR:, :] = jnp.zeros((received.shape[0], 8 - PAIR, received.shape[2]), F32)

    @pl.when(is_ocean)
    def _():
        def body(i, carry):
            greet(i // TILES, lax.rem(i + tile, TILES))
            return carry

        lax.fori_loop(0, OCEAN * TILES, body, 0)

    @pl.when(jnp.logical_not(is_ocean))
    def _():
        def body(i, carry):
            greet(OCEAN, lax.rem(i + tile, TILES))
            return carry

        lax.fori_loop(0, TILES, body, 0)

    greet(comp, left)
    greet(comp, right)

    @pl.when(has_up)
    def _():
        for t in (tile, left, right):
            greet(comp + 1, t)

    @pl.when(has_down)
    def _():
        for t in (tile, left, right):
            greet(comp - 1, t)

    load_surface.wait()
    surface = jnp.concatenate(
        [
            jnp.concatenate(
                [field[f, :, j * BLK : (j + 1) * BLK] for j in range(COLS)]
                + [jnp.zeros((64, BLK), F32)],
                axis=0,
            )
            for f in range(COUPLED)
        ],
        axis=1,
    ).astype(BF16)
    src_place = to_column(block_place(src[...].astype(F32)))
    gather = (iota((BLK, 256), 1).astype(F32) == src_place).astype(BF16)
    contrib[...] = dot(gather, surface)
    sub = iota((32, BLK), 0) % 8
    for n in range(WEIGHT_CHUNKS):
        load_weights[n].wait()

        def octet(g, carry, n=n):
            base = pl.multiple_of(n * per + g * 8, 8)
            picked = contrib[pl.ds(base, 8), :]
            lhs = jnp.concatenate(
                [picked[:, f * BLK : (f + 1) * BLK] for f in range(COUPLED)] + [jnp.zeros((8, BLK), F32)], axis=0
            )
            spread = jnp.concatenate([jnp.where(sub == k, lhs, 0.0) for k in range(8)], axis=1).astype(BF16)
            product = dot(spread, weights[pl.ds(base, 8)].reshape(8 * BLK, BLK))
            contrib[pl.ds(base, 8), :] = jnp.concatenate(
                [product[8 * f : 8 * f + 8] for f in range(COUPLED)], axis=1
            )
            return carry

        lax.fori_loop(0, per // 8, octet, 0)

    ocean_f = jnp.where(is_ocean, 1.0, 0.0)
    active = iota((1, BLK), 1) < count[0]
    tile_col = tile_of[...].astype(F32)
    tile_row = to_row(tile_col)
    same = tile_col == tile_row
    sub_i, lane_i = iota((BLK, BLK), 0), iota((BLK, BLK), 1)
    order_row = jnp.sum(jnp.where(same & (sub_i < lane_i), 1.0, 0.0), axis=0, keepdims=True)
    order_col = jnp.sum(jnp.where(same & (lane_i < sub_i), 1.0, 0.0), axis=1, keepdims=True)
    slot_iota = iota((TILES * 8, BLK), 0).astype(F32)
    place = (slot_iota == jnp.where(active, tile_row * 8.0 + order_row, -1.0)).astype(BF16)
    block = block_of[...].astype(F32)
    strip = jnp.floor((block + 0.5) * (1.0 / BLOCKS))
    code = (ocean_f * strip + (1.0 - ocean_f) * OCEAN) * BLOCKS + block_place(block - BLOCKS * strip) + 1.0
    code_high = jnp.floor(code * (1.0 / 32.0))
    code_low = code - 32.0 * code_high
    code_slot = slot_iota == jnp.where(active, tile_row * 8.0 + CAP, -1.0)
    lane_base = (lax.rem(tile, GROUP) * 8).astype(F32)
    spots = (iota((BLK, BLK), 1).astype(F32) == lane_base + order_col).astype(BF16)
    codes = 32.0 * dot(jnp.where(code_slot, code_high, 0.0).astype(BF16), spots) + dot(
        jnp.where(code_slot, code_low, 0.0).astype(BF16), spots
    )
    high, low = split(contrib[...])
    buckets = dot(place, high) + dot(place, low)
    buckets = jnp.concatenate([buckets[:, :BLK] + codes, buckets[:, BLK:]], axis=1)
    send[...] = buckets.reshape(TILES, 8, COUPLED * BLK)

    @pl.when(is_ocean)
    def _():
        pl.semaphore_wait(barrier, OCEAN * TILES + 2)

        def body(i, carry):
            t = lax.rem(i + tile, TILES)
            pltpu.make_async_remote_copy(
                src_ref=send.at[t, pl.ds(0, PAIR)],
                dst_ref=received.at[tile, pl.ds(0, PAIR)],
                send_sem=remap_send,
                recv_sem=remap_recv,
                device_id=(i // TILES, t),
                device_id_type=MESH,
            ).start()
            return carry

        lax.fori_loop(0, OCEAN * TILES, body, 0)

    @pl.when(jnp.logical_not(is_ocean))
    def _():
        sides_in = has_up.astype(jnp.int32) + has_down.astype(jnp.int32)
        pl.semaphore_wait(barrier, TILES + 2 + 3 * sides_in)

        def body(i, carry):
            t = lax.rem(i + tile, TILES)
            pltpu.make_async_remote_copy(
                src_ref=send.at[t, pl.ds(0, PAIR)],
                dst_ref=received.at[comp * TILES + tile, pl.ds(0, PAIR)],
                send_sem=remap_send,
                recv_sem=remap_recv,
                device_id=(OCEAN, t),
                device_id_type=MESH,
            ).start()
            return carry

        lax.fori_loop(0, TILES, body, 0)

    def row_copies(which):
        up = which == 0
        out = []
        for n, (a, b) in enumerate(CHUNKS):
            width = min(b, LEVELS) - a
            out.append(
                pltpu.make_async_remote_copy(
                    src_ref=state.at[pl.ds(a, width), pl.ds(BY - HALO if up else 0, HALO), :],
                    dst_ref=rows.at[pl.ds(a, width), pl.ds(HALO if up else 0, HALO), :],
                    send_sem=row_send.at[which, n],
                    recv_sem=row_recv.at[which, n],
                    device_id=(comp + 1 if up else comp - 1, tile),
                    device_id_type=MESH,
                )
            )
        out.append(
            pltpu.make_async_remote_copy(
                src_ref=kappa.at[pl.ds(BY - HALO if up else 0, HALO), :],
                dst_ref=rows.at[KAPPA, pl.ds(HALO if up else 0, HALO), :],
                send_sem=row_send.at[which, 3],
                recv_sem=row_recv.at[which, 3],
                device_id=(comp + 1 if up else comp - 1, tile),
                device_id_type=MESH,
            )
        )
        return out

    sent_up, sent_down = row_copies(0), row_copies(1)

    @pl.when(has_up)
    def _():
        sent_up[3].start()
        for copy in sent_up[:3]:
            copy.start()

    @pl.when(has_down)
    def _():
        sent_down[3].start()
        for copy in sent_down[:3]:
            copy.start()

    load_mask.wait()
    field[MASK] = mask_in[...].astype(F32)
    load_kappa.wait()
    load_state.wait()
    lane = iota((BY, BLK), 1)

    def pack_one(level, i, acc):
        here = lax.div(lane, HALO) == i
        first = pltpu.roll(field[level, :, :BLK], HALO * i, 1)
        last = pltpu.roll(field[level, :, BX - BLK :], lax.rem(HALO * i + HALO, BLK), 1)
        return jnp.where(here, first, acc[0]), jnp.where(here, last, acc[1])

    zero = jnp.zeros((BY, BLK), F32)
    for group in range(2):
        first, last = lax.fori_loop(
            0, 32 if group == 0 else MASK - 31,
            lambda i, acc, group=group: pack_one(group * 32 + i, i, acc), (zero, zero)
        )
        pack[0, group] = first
        pack[1, group] = last

    def side_copies(source, target, sems):
        out = []
        for side, there in ((0, left), (1, right)):
            for vertical in (0, 1, 2):
                if vertical == 0:
                    cond, c, here_rows, there_rows = None, comp, (0, BY), (0, BY)
                elif vertical == 1:
                    cond, c, here_rows, there_rows = has_up, comp + 1, (BY - HALO, HALO), (BY + HALO, HALO)
                else:
                    cond, c, here_rows, there_rows = has_down, comp - 1, (0, HALO), (BY, HALO)
                out.append((
                    cond,
                    pltpu.make_async_remote_copy(
                        src_ref=source.at[side, :, pl.ds(*here_rows), :],
                        dst_ref=target.at[side, :, pl.ds(*there_rows), :],
                        send_sem=sems.at[0, side, vertical],
                        recv_sem=sems.at[1, side, vertical],
                        device_id=(c, there),
                        device_id_type=MESH,
                    ),
                ))
        return out

    def start_sides(copies):
        for cond, copy in copies:
            if cond is None:
                copy.start()
            else:
                pl.when(cond)(copy.start)

    def wait_sides(copies):
        for n, (cond, copy) in enumerate(copies):
            if cond is None:
                copy.wait_recv()
            else:
                pl.when(has_down if n % 3 == 1 else has_up)(copy.wait_recv)

    def wait_sent(copies):
        for cond, copy in copies:
            if cond is None:
                copy.wait_send()
            else:
                pl.when(cond)(copy.wait_send)

    early = side_copies(pack, sides, side_sem)
    start_sides(early)
    wait_sides(early)

    @pl.when(comp == 0)
    def _():
        for k in range(HALO):
            sides[:, :, pl.ds(BY + 2 * HALO - 1 - k, 1), :] = sides[:, :, pl.ds(k, 1), :]
            rows[pl.ds(COUPLED, KAPPA + 1 - COUPLED), pl.ds(2 * HALO - 1 - k, 1), :] = field[
                pl.ds(COUPLED, KAPPA + 1 - COUPLED), pl.ds(k, 1), :
            ]

    @pl.when(comp == OCEAN - 1)
    def _():
        for k in range(HALO):
            sides[:, :, pl.ds(BY + k, 1), :] = sides[:, :, pl.ds(BY - 1 - k, 1), :]
            rows[pl.ds(COUPLED, KAPPA + 1 - COUPLED), pl.ds(k, 1), :] = field[
                pl.ds(COUPLED, KAPPA + 1 - COUPLED), pl.ds(BY - 1 - k, 1), :
            ]

    def wait_rows(n):
        pl.when(has_down)(sent_up[n].wait_recv)
        pl.when(has_up)(sent_down[n].wait_recv)

    wait_rows(3)

    @pl.when(is_ocean)
    def _():
        m = jnp.concatenate(
            [field[MASK], edge_tile(sides[0, 1], sides[1, 1], MASK - 32)[:BY]], axis=1
        )
        k = jnp.concatenate(
            [field[KAPPA], edge_tile(sides[0, 1], sides[1, 1], KAPPA - 32)[:BY]], axis=1
        )
        open_right = m * pltpu.roll(m, WIDE - 1, 1)
        row = iota((BY, WIDE), 0)
        open_up = jnp.where(row == BY - 1, 0.0, m * pltpu.roll(m, BY - 1, 0))
        k_right = k * open_right
        k_left = k * pltpu.roll(open_right, 1, 1)
        k_up = k * open_up
        k_down = k * pltpu.roll(open_up, 1, 0)
        coef[0, :BY] = 1.0 - ((k_right + k_left) + (k_up + k_down))
        coef[1, :BY] = k_right
        coef[2, :BY] = k_left
        coef[3, :BY] = k_up
        coef[4, :BY] = k_down

    @pl.when(jnp.logical_not(is_ocean))
    def _():
        k = jnp.concatenate([field[KAPPA], rows[KAPPA]], axis=0)
        k = jnp.concatenate([k, edge_tile(sides[0, 1], sides[1, 1], KAPPA - 32)], axis=1)
        coef[0] = 1.0 - 4.0 * k
        coef[1] = k

    def diffuse(start, stop):
        @pl.when(is_ocean)
        def _():
            diffuse_levels(True, field, rows, sides, coef, start, stop, field)

        @pl.when(jnp.logical_not(is_ocean))
        def _():
            diffuse_levels(False, field, rows, sides, coef, start, stop, field)

    at = COUPLED
    for n, (a, b) in enumerate(CHUNKS):
        wait_rows(n)
        stop = min(b, FIRST)
        if at < stop:
            diffuse(at, stop)
            at = stop

    def accumulate(sources):
        pltpu.make_async_copy(
            received.at[pl.ds(0, sources), pl.ds(0, PAIR)],
            received.at[pl.ds(0, sources), pl.ds(0, PAIR)],
            remap_recv,
        ).wait()
        heads = received[pl.ds(0, sources), CAP, :BLK]
        offset = 1.0 + BLOCKS * comp.astype(F32)
        total = jnp.zeros((BLOCKS, COUPLED * BLK), F32)
        for g in range(sources // GROUP):
            codes_in = jnp.sum(heads[GROUP * g : GROUP * g + GROUP], axis=0, keepdims=True) - offset
            codes_in = codes_in[:, : GROUP * 8]
            onehot = (iota((BLOCKS, GROUP * 8), 0).astype(F32) == codes_in).astype(BF16)
            values = received[pl.ds(GROUP * g, GROUP)].reshape(GROUP * 8, COUPLED * BLK)
            big, small = split(values)
            total = total + dot(onehot, big) + dot(onehot, small)
        for f in range(COUPLED):
            for j in range(COLS):
                cut = (f, slice(None), slice(j * BLK, (j + 1) * BLK))
                old = field[cut]
                new = total[j * BY : (j + 1) * BY, f * BLK : (f + 1) * BLK]
                field[cut] = old + 0.5 * field[MASK, :, j * BLK : (j + 1) * BLK] * (new - old)

    pl.when(is_ocean)(lambda: accumulate(OCEAN * TILES))
    pl.when(jnp.logical_not(is_ocean))(lambda: accumulate(TILES))

    late_up = pltpu.make_async_remote_copy(
        src_ref=field.at[pl.ds(0, COUPLED), pl.ds(BY - HALO, HALO), :],
        dst_ref=rows.at[pl.ds(0, COUPLED), pl.ds(HALO, HALO), :],
        send_sem=row_send.at[0, 4],
        recv_sem=row_recv.at[0, 4],
        device_id=(comp + 1, tile),
        device_id_type=MESH,
    )
    late_down = pltpu.make_async_remote_copy(
        src_ref=field.at[pl.ds(0, COUPLED), pl.ds(0, HALO), :],
        dst_ref=rows.at[pl.ds(0, COUPLED), pl.ds(0, HALO), :],
        send_sem=row_send.at[1, 4],
        recv_sem=row_recv.at[1, 4],
        device_id=(comp - 1, tile),
        device_id_type=MESH,
    )
    pl.when(has_up)(late_up.start)
    pl.when(has_down)(late_down.start)
    acc = (zero, zero)
    for level in range(COUPLED):
        acc = pack_one(level, level, acc)
    late_pack[0, 0] = acc[0]
    late_pack[1, 0] = acc[1]
    late = side_copies(late_pack, late_sides, late_sem)
    start_sides(late)

    if at < LEVELS:
        diffuse(at, LEVELS)

    wait_sides(late)
    pl.when(has_down)(late_up.wait_recv)
    pl.when(has_up)(late_down.wait_recv)

    @pl.when(comp == 0)
    def _():
        for k in range(HALO):
            late_sides[:, :, pl.ds(BY + 2 * HALO - 1 - k, 1), :] = late_sides[:, :, pl.ds(k, 1), :]
            rows[pl.ds(0, COUPLED), pl.ds(2 * HALO - 1 - k, 1), :] = field[pl.ds(0, COUPLED), pl.ds(k, 1), :]

    @pl.when(comp == OCEAN - 1)
    def _():
        for k in range(HALO):
            late_sides[:, :, pl.ds(BY + k, 1), :] = late_sides[:, :, pl.ds(BY - 1 - k, 1), :]
            rows[pl.ds(0, COUPLED), pl.ds(k, 1), :] = field[pl.ds(0, COUPLED), pl.ds(BY - 1 - k, 1), :]

    wait_sent(early)
    wait_sent(late)

    @pl.when(has_up)
    def _():
        for copy in sent_up:
            copy.wait_send()
        late_up.wait_send()

    @pl.when(has_down)
    def _():
        for copy in sent_down:
            copy.wait_send()
        late_down.wait_send()

    @pl.when(is_ocean)
    def _():
        whole = received.at[:, pl.ds(0, PAIR)]
        pltpu.make_async_copy(whole, whole, remap_send).wait()

    @pl.when(jnp.logical_not(is_ocean))
    def _():
        whole = received.at[pl.ds(0, TILES), pl.ds(0, PAIR)]
        pltpu.make_async_copy(whole, whole, remap_send).wait()


def finish_kernel(field, rows, late_sides, coef, out, done, sem):
    is_ocean = lax.axis_index("comp") == OCEAN
    rest = pltpu.make_async_copy(
        field.at[pl.ds(COUPLED, LEVELS - COUPLED)], out.at[pl.ds(COUPLED, LEVELS - COUPLED)], sem.at[0]
    )
    rest.start()

    def surface(ocean):
        for level in range(COUPLED):
            done[level] = level_steps(
                ocean, field, rows, late_sides[0, 0], late_sides[1, 0], coef, level, level
            )

    pl.when(is_ocean)(lambda: surface(True))
    pl.when(jnp.logical_not(is_ocean))(lambda: surface(False))
    head = pltpu.make_async_copy(done, out.at[pl.ds(0, COUPLED)], sem.at[1])
    head.start()
    head.wait()
    rest.wait()


def shards(state, kappa, land_mask, remap_weight, remap_src, remap_tile, remap_block, remap_count):
    vmem = pl.BlockSpec(memory_space=pltpu.VMEM)
    hbm = pl.BlockSpec(memory_space=pltpu.HBM)
    tall = BY + 2 * HALO
    kept = (
        pltpu.VMEM((HELD, BY, BX), F32),
        pltpu.VMEM((KAPPA + 1, 2 * HALO, BX), F32),
        pltpu.VMEM((2, 1, tall, BLK), F32),
        pltpu.VMEM((5, tall, WIDE), F32),
    )
    field, rows, late_sides, coef = pl.pallas_call(
        exchange_kernel,
        out_shape=kept,
        in_specs=[hbm, hbm, hbm, hbm, vmem, vmem, vmem, pl.BlockSpec(memory_space=pltpu.SMEM)],
        out_specs=(vmem,) * 4,
        scratch_shapes=[
            pltpu.VMEM((2, 2, tall, BLK), F32),
            pltpu.VMEM((SLOTS, BLK, BLK), BF16),
            pltpu.VMEM((BY, BX), jnp.int32),
            pltpu.VMEM((TILES, 8, COUPLED * BLK), F32),
            pltpu.VMEM((OCEAN * TILES, 8, COUPLED * BLK), F32),
            pltpu.VMEM((SLOTS, COUPLED * BLK), F32),
            pltpu.VMEM((2, 2, BY, BLK), F32),
            pltpu.VMEM((2, 1, BY, BLK), F32),
            pltpu.SemaphoreType.DMA((3,)),
            pltpu.SemaphoreType.DMA((WEIGHT_CHUNKS,)),
            pltpu.SemaphoreType.DMA,
            pltpu.SemaphoreType.DMA,
            pltpu.SemaphoreType.DMA,
            pltpu.SemaphoreType.DMA((2, 5)),
            pltpu.SemaphoreType.DMA((2, 5)),
            pltpu.SemaphoreType.DMA((2, 2, 3)),
            pltpu.SemaphoreType.DMA((2, 2, 3)),
        ],
        compiler_params=pltpu.CompilerParams(
            collective_id=0, has_side_effects=True, vmem_limit_bytes=32 << 20
        ),
        name="exchange",
    )(
        *(pltpu.with_memory_space_constraint(x, pltpu.HBM) for x in (state, kappa, land_mask, remap_weight)),
        remap_src.reshape(1, SLOTS), remap_tile, remap_block.reshape(1, SLOTS), remap_count,
    )
    return pl.pallas_call(
        finish_kernel,
        out_shape=jax.ShapeDtypeStruct((LEVELS, BY, BX), F32),
        in_specs=[vmem] * 4,
        out_specs=hbm,
        scratch_shapes=[pltpu.VMEM((COUPLED, BY, BX), F32), pltpu.SemaphoreType.DMA((2,))],
        compiler_params=pltpu.CompilerParams(vmem_limit_bytes=24 << 20),
        name="finish",
    )(field, rows, late_sides, coef)


def solution(mesh):
    return jax.shard_map(
        shards,
        mesh=mesh,
        in_specs=(
            P(None, "comp", "tile"),
            P("comp", "tile"),
            P("comp", "tile"),
            P(("comp", "tile"), None, None),
            P(("comp", "tile")),
            P(("comp", "tile"), None),
            P(("comp", "tile")),
            P(("comp", "tile")),
        ),
        out_specs=P(None, "comp", "tile"),
        check_vma=False,
    )
```

```python
import jax
import jax.numpy as jnp
from jax import lax
from jax.experimental import pallas as pl
from jax.experimental.pallas import tpu as pltpu
from jax.sharding import PartitionSpec as P

LEVELS = 60
COUPLED = 3
DEEP = LEVELS - COUPLED
BLK = 128
BY = 32
BX = 768
HALO = 4
TALL = BY + 2 * HALO
TOP = HALO + BY
SLOTS = 128
CAP = 6
PAIR = 7
TILES = 32
OCEAN = 3
BLOCKS = 192
COLS = BX // BLK
HALF = COLS // 2
WIDE = BX + BLK
KAPPA, SEA = 3, 4
LANES = 64
FIRST = 8
LAST = FIRST + HALF * BLK
LONG = LAST + 8
STRIDE = 49
WEIGHT_CHUNKS = 4
GROUP = min(16, TILES)
MESH = pl.DeviceIdType.MESH
F32 = jnp.float32
BF16 = jnp.bfloat16


def iota(shape, axis):
    return lax.broadcasted_iota(jnp.int32, shape, axis)


def split(x):
    high = x.astype(BF16)
    return high, (x - high.astype(F32)).astype(BF16)


def dot(a, b):
    return jnp.dot(a, b, preferred_element_type=F32)


def to_column(row):
    eye = iota((BLK, BLK), 0) == iota((BLK, BLK), 1)
    return jnp.sum(jnp.where(eye, row, 0.0), axis=1, keepdims=True)


def block_place(block):
    row = jnp.floor((block + 0.5) * (1.0 / COLS))
    return (block - COLS * row) * BY + row


def own(ref, *lead):
    return ref[lead + (pl.ds(HALO, BY), slice(None))]


def level_rows(slab, group, y):
    return pl.ds((slab * LANES + group * 8) * TALL + y, 8, stride=TALL)


def as_rows(ref):
    return ref.reshape(COLS * LANES * TALL, BLK)


def wide(ref, *lead):
    return jnp.concatenate([ref[lead + (j,)] for j in range(COLS + 1)], axis=1)


def neighbours(v):
    return (pltpu.roll(v, 1, 1) + pltpu.roll(v, WIDE - 1, 1)) + (
        pltpu.roll(v, 1, 0) + pltpu.roll(v, TALL - 1, 0)
    )


def step_rows(old, new, around, centre, y0, count):
    def load(ref, y, i):
        return ref[y0 + y, pl.ds(HALO + i, 8, stride=STRIDE), :]

    def one(i, carry):
        here, before = carry
        ahead = [load(old, y, i + 1) for y in range(-1, count + 1)]
        diagonal = [here[y] + ahead[y + 1] for y in range(count + 1)]
        for y in range(count):
            near = before[y] + diagonal[y]
            new[y0 + y, pl.ds(HALO + i, 8, stride=STRIDE), :] = (
                load(centre, y, i) * here[y + 1] + load(around, y, i) * near
            )
        return ahead, diagonal[1:]

    behind = [load(old, y, -1) for y in range(count)]
    here = [load(old, y, 0) for y in range(-1, count + 1)]
    before = [behind[y] + here[y + 2] for y in range(count)]
    lax.fori_loop(0, STRIDE, one, (here, before), unroll=7)


def step_blocks(old, new, around, centre, start, count, last, blocks):
    def one(b, carry):
        step_rows(old, new, around, centre, jnp.minimum(start + count * b, last), count)
        return carry

    lax.fori_loop(*blocks, one, 0)


def exchange_kernel(
    state, kappa, mask, weight, src, tile_of, block_of, count,
    natural, planes, sides, coef, field, around, centre,
    other, ends, weights, mask_in, small, send, received, contrib,
    load_sem, weight_sem, state_sem, remap_send, remap_recv, row_sem, side_sem,
):
    comp = lax.axis_index("comp")
    tile = lax.axis_index("tile")
    right = lax.rem(tile + 1, TILES)
    left = lax.rem(tile + TILES - 1, TILES)
    is_ocean = comp == OCEAN
    has_up = comp < OCEAN - 1
    has_down = (comp > 0) & (comp < OCEAN)

    loads = [
        pltpu.make_async_copy(part, small.at[n], load_sem.at[n])
        for n, part in enumerate((src, tile_of, block_of))
    ]
    surface_loads, kappa_loads, state_loads = [], [], []
    for j in range(COLS):
        cut = pl.ds(j * BLK, BLK)
        surface_loads.append(
            pltpu.make_async_copy(
                state.at[pl.ds(0, COUPLED), :, cut],
                planes.at[pl.ds(0, COUPLED), j, pl.ds(HALO, BY), :],
                load_sem.at[4 + j],
            )
        )
        kappa_loads.append(
            pltpu.make_async_copy(
                kappa.at[:, cut], planes.at[KAPPA, j, pl.ds(HALO, BY), :], load_sem.at[10 + j]
            )
        )
        state_loads.append(
            pltpu.make_async_copy(
                state.at[pl.ds(COUPLED, DEEP), :, cut],
                natural.at[j, pl.ds(0, DEEP), pl.ds(0, BY), :],
                state_sem.at[j],
            )
        )
    mask_load = pltpu.make_async_copy(mask, mask_in, load_sem.at[16])
    per = SLOTS // WEIGHT_CHUNKS
    weight_loads = [
        pltpu.make_async_copy(weight.at[pl.ds(n * per, per)], weights.at[pl.ds(n * per, per)], weight_sem.at[n])
        for n in range(WEIGHT_CHUNKS)
    ]
    for copy in loads + surface_loads + weight_loads + kappa_loads + [mask_load] + state_loads:
        copy.start()

    barrier = pltpu.get_barrier_semaphore()

    def greet(c, t):
        pl.semaphore_signal(barrier, inc=1, device_id=(c, t), device_id_type=MESH)

    greet(comp, left)
    greet(comp, right)

    @pl.when(has_up)
    def _():
        for t in (tile, left, right):
            greet(comp + 1, t)

    @pl.when(has_down)
    def _():
        for t in (tile, left, right):
            greet(comp - 1, t)

    @pl.when(is_ocean)
    def _():
        def body(i, carry):
            greet(i // TILES, lax.rem(i + tile, TILES))
            return carry

        lax.fori_loop(0, OCEAN * TILES, body, 0)

    @pl.when(jnp.logical_not(is_ocean))
    def _():
        def body(i, carry):
            greet(OCEAN, lax.rem(i + tile, TILES))
            return carry

        lax.fori_loop(0, TILES, body, 0)

    received[:, PAIR:, :] = jnp.zeros((received.shape[0], 8 - PAIR, received.shape[2]), F32)

    for copy in loads + surface_loads:
        copy.wait()
    surface = jnp.concatenate(
        [
            jnp.concatenate(
                [own(planes, f, j) for j in range(COLS)] + [jnp.zeros((64, BLK), F32)], axis=0
            )
            for f in range(COUPLED)
        ],
        axis=1,
    ).astype(BF16)
    src_place = to_column(block_place(small[0].astype(F32)))
    gather = (iota((BLK, 256), 1).astype(F32) == src_place).astype(BF16)
    picked_all = dot(gather, surface)
    sub = iota((32, BLK), 0) % 8
    for n in range(WEIGHT_CHUNKS):
        weight_loads[n].wait()
        for g in range(per // 8):
            base = n * per + g * 8
            picked = picked_all[base : base + 8]
            lhs = jnp.concatenate(
                [picked[:, f * BLK : (f + 1) * BLK] for f in range(COUPLED)] + [jnp.zeros((8, BLK), F32)], axis=0
            )
            spread = jnp.concatenate([jnp.where(sub == k, lhs, 0.0) for k in range(8)], axis=1).astype(BF16)
            product = dot(spread, weights[pl.ds(base, 8)].reshape(8 * BLK, BLK))
            for f in range(COUPLED):
                contrib[pl.ds(base, 8), f * BLK : (f + 1) * BLK] = product[8 * f : 8 * f + 8]

    ocean_f = jnp.where(is_ocean, 1.0, 0.0)
    active = iota((1, BLK), 1) < count[0]
    tile_row = small[1].astype(F32)
    tile_col = to_column(tile_row)
    same = tile_col == tile_row
    sub_i, lane_i = iota((BLK, BLK), 0), iota((BLK, BLK), 1)
    order_row = jnp.sum(jnp.where(same & (sub_i < lane_i), 1.0, 0.0), axis=0, keepdims=True)
    order_col = jnp.sum(jnp.where(same & (lane_i < sub_i), 1.0, 0.0), axis=1, keepdims=True)
    slot_iota = iota((TILES * 8, BLK), 0).astype(F32)
    place = (slot_iota == jnp.where(active, tile_row * 8.0 + order_row, -1.0)).astype(BF16)
    block = small[2].astype(F32)
    strip = jnp.floor((block + 0.5) * (1.0 / BLOCKS))
    code = (ocean_f * strip + (1.0 - ocean_f) * OCEAN) * BLOCKS + block_place(block - BLOCKS * strip) + 1.0
    code_high = jnp.floor(code * (1.0 / 32.0))
    code_low = code - 32.0 * code_high
    code_slot = slot_iota == jnp.where(active, tile_row * 8.0 + CAP, -1.0)
    lane_base = (lax.rem(tile, GROUP) * 8).astype(F32)
    spots = (iota((BLK, BLK), 1).astype(F32) == lane_base + order_col).astype(BF16)
    codes = 32.0 * dot(jnp.where(code_slot, code_high, 0.0).astype(BF16), spots) + dot(
        jnp.where(code_slot, code_low, 0.0).astype(BF16), spots
    )
    high, low = split(contrib[...])
    buckets = dot(place, high) + dot(place, low)
    buckets = jnp.concatenate([buckets[:, :BLK] + codes, buckets[:, BLK:]], axis=1)
    send[...] = buckets.reshape(TILES, 8, COUPLED * BLK)

    for copy in kappa_loads:
        copy.wait()
    mask_load.wait()
    row = iota((TALL, BLK), 0)
    beyond = ((row < HALO) & jnp.logical_not(has_down)) | ((row >= TOP) & jnp.logical_not(has_up))
    inside = jnp.where(beyond, 0.0, 1.0)
    for j in range(COLS):
        planes[SEA, j] = inside
        planes[SEA, j, pl.ds(HALO, BY), :] = jnp.maximum(
            mask_in[:, j * BLK : (j + 1) * BLK].astype(F32), 1.0 - ocean_f
        )

    sides_in = has_up.astype(jnp.int32) + has_down.astype(jnp.int32)
    pl.semaphore_wait(barrier, jnp.where(is_ocean, OCEAN * TILES + 2, TILES + 2 + 3 * sides_in))

    def remote(source, target, sems, n, device):
        return pltpu.make_async_remote_copy(
            src_ref=source,
            dst_ref=target,
            send_sem=sems.at[0, n],
            recv_sem=sems.at[1, n],
            device_id=device,
            device_id_type=MESH,
        )

    def row_copies(cut, sems, n):
        return [
            (has_up, has_down, remote(cut(TOP - HALO), cut(0), sems, n, (comp + 1, tile))),
            (has_down, has_up, remote(cut(HALO), cut(TOP), sems, n + 1, (comp - 1, tile))),
        ]

    def column_copies(source, target, sems, n):
        out = []
        for side, there in ((0, left), (1, right)):
            out += [
                (None, None, remote(source(side, HALO, BY), target(side, HALO, BY), sems, n, (comp, there))),
                (has_up, has_down, remote(
                    source(side, TOP - HALO, HALO), target(side, 0, HALO), sems, n + 1, (comp + 1, there))),
                (has_down, has_up, remote(
                    source(side, HALO, HALO), target(side, TOP, HALO), sems, n + 2, (comp - 1, there))),
            ]
            n += 3
        return out

    def each(copies, pick, act):
        for entry in copies:
            cond, copy = entry[pick], entry[2]
            if cond is None:
                act(copy)()
            else:
                pl.when(cond)(act(copy))

    def start(copies):
        each(copies, 0, lambda copy: copy.start)

    def wait_recv(copies):
        each(copies, 1, lambda copy: copy.wait_recv)

    def wait_send(copies):
        each(copies, 0, lambda copy: copy.wait_send)

    def plane_rows(first, number):
        return lambda y: planes.at[pl.ds(first, number), pl.ds(0, COLS), pl.ds(y, HALO), :]

    def plane_edge(first, number):
        return lambda side, y, rows: planes.at[pl.ds(first, number), side * (COLS - 1), pl.ds(y, rows), :]

    def side_edge(first, number):
        return lambda side, y, rows: sides.at[side, pl.ds(first, number), pl.ds(y, rows), :]

    early = row_copies(plane_rows(KAPPA, 1), row_sem, 0) + column_copies(
        plane_edge(KAPPA, 2), side_edge(KAPPA, 2), side_sem, 0
    )
    start(early)

    @pl.when(is_ocean)
    def _():
        def body(i, carry):
            t = lax.rem(i + tile, TILES)
            pltpu.make_async_remote_copy(
                src_ref=send.at[t, pl.ds(0, PAIR)],
                dst_ref=received.at[tile, pl.ds(0, PAIR)],
                send_sem=remap_send,
                recv_sem=remap_recv,
                device_id=(i // TILES, t),
                device_id_type=MESH,
            ).start()
            return carry

        lax.fori_loop(0, OCEAN * TILES, body, 0)

    @pl.when(jnp.logical_not(is_ocean))
    def _():
        def body(i, carry):
            t = lax.rem(i + tile, TILES)
            pltpu.make_async_remote_copy(
                src_ref=send.at[t, pl.ds(0, PAIR)],
                dst_ref=received.at[comp * TILES + tile, pl.ds(0, PAIR)],
                send_sem=remap_send,
                recv_sem=remap_recv,
                device_id=(OCEAN, t),
                device_id_type=MESH,
            ).start()
            return carry

        lax.fori_loop(0, TILES, body, 0)

    for copy in state_loads:
        copy.wait()
    flat = as_rows(natural)

    def turn(y):
        for j in range(HALF):
            parts = []
            for slab in (j, j + HALF):
                sea = planes[SEA, slab, pl.ds(HALO + y, 1), :] > 0.0
                for g in range(LANES // 8):
                    levels = flat[level_rows(slab, g, y), :]
                    parts.append(jnp.where(sea, levels, 0.0))
            field[HALO + y, pl.ds(FIRST + j * BLK, BLK), :] = jnp.concatenate(parts, axis=0).T

    def outer(i, carry):
        turn(jnp.where(i < HALO, i, i + BY - 2 * HALO))
        return carry

    def inner(i, carry):
        turn(i + HALO)
        return carry

    lax.fori_loop(0, 2 * HALO, outer, 0, unroll=4)
    deep_rows = row_copies(
        lambda y: field.at[pl.ds(y, HALO), pl.ds(FIRST, HALF * BLK), :], row_sem, 2
    )
    start(deep_rows)
    lax.fori_loop(0, BY - 2 * HALO, inner, 0, unroll=4)
    deep_sides = column_copies(
        lambda side, y, rows: field.at[pl.ds(y, rows), pl.ds(LAST - HALO if side else FIRST, HALO), :],
        lambda side, y, rows: ends.at[side, pl.ds(y, rows), pl.ds(HALO if side else 0, HALO), :],
        side_sem, 6,
    )
    start(deep_sides)

    wait_recv(early)
    lane = iota((TALL, BLK), 1)
    for side in range(2):
        sides[side, SEA, pl.ds(0, HALO), :] = inside[:HALO]
        sides[side, SEA, pl.ds(TOP, HALO), :] = inside[TOP:]
    for p in (KAPPA, SEA):
        planes[p, COLS] = jnp.where(lane < BLK // 2, sides[0, p], sides[1, p])
    sea = wide(planes, SEA)
    scale = jnp.where(sea > 0.0, wide(planes, KAPPA), 0.0)
    middle = 1.0 - scale * neighbours(sea)
    for n, value in enumerate((middle, scale)):
        tiles = [value[:, j * BLK : (j + 1) * BLK] for j in range(COLS + 1)]
        for j in range(COLS + 1):
            coef[n, j] = tiles[j]
        coef[n, COLS + 1] = jnp.where(lane < BLK // 2, tiles[HALF], tiles[COLS])
        coef[n, COLS + 2] = jnp.where(lane < BLK // 2, tiles[COLS], tiles[HALF - 1])

    def spread_row(y, carry):
        for n, target in enumerate((centre, around)):
            for a, b, at in [(j, j + HALF, FIRST + j * BLK) for j in range(HALF)] + [(COLS + 1, COLS + 2, None)]:
                both = jnp.concatenate(
                    [
                        jnp.broadcast_to(coef[n, a, pl.ds(y, 1), :], (LANES, BLK)),
                        jnp.broadcast_to(coef[n, b, pl.ds(y, 1), :], (LANES, BLK)),
                    ],
                    axis=0,
                ).T
                if at is None:
                    target[y, pl.ds(LAST, 8), :] = both[:8]
                    target[y, pl.ds(0, 8), :] = both[BLK - 8 :]
                else:
                    target[y, pl.ds(at, BLK), :] = both
        return carry

    lax.fori_loop(0, TALL, spread_row, 0, unroll=2)

    def join(y, carry):
        low = iota((8, BLK), 1) < LANES
        first = field[y, pl.ds(FIRST, 8), :]
        last = field[y, pl.ds(LAST - 8, 8), :]
        field[y, pl.ds(LAST, 8), :] = pltpu.roll(jnp.where(low, ends[0, y], first), LANES, 1)
        field[y, pl.ds(0, 8), :] = pltpu.roll(jnp.where(low, last, ends[1, y]), LANES, 1)
        return carry

    wait_recv(deep_sides)
    lax.fori_loop(HALO, TOP, join, 0, unroll=4)
    step_blocks(field, other, around, centre, 1, 10, 29, (1, 3))
    wait_recv(deep_rows)

    @pl.when(jnp.logical_not(has_down))
    def _():
        field[pl.ds(0, HALO)] = jnp.zeros((HALO, LONG, BLK), F32)

    @pl.when(jnp.logical_not(has_up))
    def _():
        field[pl.ds(TOP, HALO)] = jnp.zeros((HALO, LONG, BLK), F32)

    @pl.when(has_down)
    def _():
        lax.fori_loop(0, HALO, join, 0, unroll=4)

    @pl.when(has_up)
    def _():
        lax.fori_loop(TOP, TALL, join, 0, unroll=4)

    step_blocks(field, other, around, centre, 1, 10, 29, (0, 1))
    step_blocks(field, other, around, centre, 1, 10, 29, (3, 4))
    wait_send(deep_rows)
    wait_send(deep_sides)
    step_blocks(other, field, around, centre, 2, 9, 29, (0, 4))

    def accumulate(sources):
        whole = received.at[pl.ds(0, sources), pl.ds(0, PAIR)]
        pltpu.make_async_copy(whole, whole, remap_recv).wait()
        heads = received[pl.ds(0, sources), CAP, :BLK]
        offset = 1.0 + BLOCKS * comp.astype(F32)
        total = jnp.zeros((BLOCKS, COUPLED * BLK), F32)
        for g in range(sources // GROUP):
            codes_in = jnp.sum(heads[GROUP * g : GROUP * g + GROUP], axis=0, keepdims=True) - offset
            codes_in = codes_in[:, : GROUP * 8]
            onehot = (iota((BLOCKS, GROUP * 8), 0).astype(F32) == codes_in).astype(BF16)
            values = received[pl.ds(GROUP * g, GROUP)].reshape(GROUP * 8, COUPLED * BLK)
            big, little = split(values)
            total = total + dot(onehot, big) + dot(onehot, little)
        for j in range(COLS):
            weight_here = 0.5 * mask_in[:, j * BLK : (j + 1) * BLK].astype(F32)
            for f in range(COUPLED):
                old = own(planes, f, j)
                new = total[j * BY : (j + 1) * BY, f * BLK : (f + 1) * BLK]
                planes[f, j, pl.ds(HALO, BY), :] = old + weight_here * (new - old)

    pl.when(is_ocean)(lambda: accumulate(OCEAN * TILES))
    pl.when(jnp.logical_not(is_ocean))(lambda: accumulate(TILES))

    late = row_copies(plane_rows(0, COUPLED), row_sem, 4) + column_copies(
        plane_edge(0, COUPLED), side_edge(0, COUPLED), side_sem, 12
    )
    start(late)
    step_blocks(field, other, around, centre, 3, 9, 28, (0, 4))
    wait_recv(late)

    wait_send(early)
    wait_send(late)

    @pl.when(is_ocean)
    def _():
        whole = received.at[:, pl.ds(0, PAIR)]
        pltpu.make_async_copy(whole, whole, remap_send).wait()

    @pl.when(jnp.logical_not(is_ocean))
    def _():
        whole = received.at[pl.ds(0, TILES), pl.ds(0, PAIR)]
        pltpu.make_async_copy(whole, whole, remap_send).wait()

    step_blocks(other, field, around, centre, HALO, 8, 28, (0, 4))


def finish_kernel(natural, planes, sides, coef, field, out, result, done, sem):
    flat, flat_result = as_rows(natural), as_rows(result)
    copies = []
    for j in range(HALF):

        def turn(y, carry, j=j):
            back = field[HALO + y, pl.ds(FIRST + j * BLK, BLK), :].T
            for h, slab in enumerate((j, j + HALF)):
                sea = planes[SEA, slab, pl.ds(HALO + y, 1), :] > 0.0
                for g in range(LANES // 8):
                    at = level_rows(slab, g, y)
                    piece = back[h * LANES + g * 8 : h * LANES + g * 8 + 8]
                    flat_result[at, :] = jnp.where(sea, piece, flat[at, :])
            return carry

        lax.fori_loop(0, BY, turn, 0, unroll=8)
        for slab in (j, j + HALF):
            copies.append(
                pltpu.make_async_copy(
                    result.at[slab, pl.ds(0, DEEP), pl.ds(0, BY), :],
                    out.at[pl.ds(COUPLED, DEEP), :, pl.ds(slab * BLK, BLK)],
                    sem.at[slab],
                )
            )
            copies[-1].start()

    lane = iota((TALL, BLK), 1)
    sea = wide(planes, SEA) > 0.0
    middle, scale = wide(coef, 0), wide(coef, 1)
    for f in range(COUPLED):
        edge = jnp.where(lane < BLK // 2, sides[0, f], sides[1, f])
        v = jnp.concatenate([planes[f, j] for j in range(COLS)] + [edge], axis=1)
        w = jnp.where(sea, v, 0.0)
        for _ in range(4):
            w = middle * w + scale * neighbours(w)
        done[f] = jnp.where(sea, w, v)[HALO:TOP, :BX]
    copies.append(pltpu.make_async_copy(done, out.at[pl.ds(0, COUPLED)], sem.at[COLS]))
    copies[-1].start()
    for copy in copies:
        copy.wait()


def shards(state, kappa, land_mask, remap_weight, remap_src, remap_tile, remap_block, remap_count):
    vmem = pl.BlockSpec(memory_space=pltpu.VMEM)
    hbm = pl.BlockSpec(memory_space=pltpu.HBM)
    kept = (
        pltpu.VMEM((COLS, LANES, TALL, BLK), F32),
        pltpu.VMEM((5, COLS + 1, TALL, BLK), F32),
        pltpu.VMEM((2, 5, TALL, BLK), F32),
        pltpu.VMEM((2, COLS + 3, TALL, BLK), F32),
        pltpu.VMEM((TALL, LONG, BLK), F32),
    )
    operands = (
        state, kappa, land_mask, remap_weight,
        remap_src.reshape(1, SLOTS), remap_tile.reshape(1, SLOTS),
        remap_block.reshape(1, SLOTS),
    )
    dma = pltpu.SemaphoreType.DMA
    natural, planes, sides, coef, field = pl.pallas_call(
        exchange_kernel,
        out_shape=kept,
        in_specs=[hbm] * 7 + [pl.BlockSpec(memory_space=pltpu.SMEM)],
        out_specs=(vmem,) * len(kept),
        scratch_shapes=[
            pltpu.VMEM((TALL, LONG, BLK), F32),
            pltpu.VMEM((TALL, LONG, BLK), F32),
            pltpu.VMEM((TALL, LONG, BLK), F32),
            pltpu.VMEM((2, TALL, 8, BLK), F32),
            pltpu.VMEM((SLOTS, BLK, BLK), BF16),
            pltpu.VMEM((BY, BX), jnp.int32),
            pltpu.VMEM((3, 1, SLOTS), jnp.int32),
            pltpu.VMEM((TILES, 8, COUPLED * BLK), F32),
            pltpu.VMEM((OCEAN * TILES, 8, COUPLED * BLK), F32),
            pltpu.VMEM((SLOTS, COUPLED * BLK), F32),
            dma((17,)),
            dma((WEIGHT_CHUNKS,)),
            dma((COLS,)),
            dma,
            dma,
            dma((2, 6)),
            dma((2, 18)),
        ],
        compiler_params=pltpu.CompilerParams(
            collective_id=0, has_side_effects=True, vmem_limit_bytes=36 << 20
        ),
        name="exchange",
    )(*(pltpu.with_memory_space_constraint(x, pltpu.HBM) for x in operands), remap_count)
    return pl.pallas_call(
        finish_kernel,
        out_shape=jax.ShapeDtypeStruct((LEVELS, BY, BX), F32),
        in_specs=[vmem] * len(kept),
        out_specs=hbm,
        scratch_shapes=[pltpu.VMEM((COLS, LANES, TALL, BLK), F32), pltpu.VMEM((COUPLED, BY, BX), F32), dma((COLS + 1,))],
        compiler_params=pltpu.CompilerParams(vmem_limit_bytes=16 << 20),
        name="finish",
    )(natural, planes, sides, coef, field)


def solution(mesh):
    return jax.shard_map(
        shards,
        mesh=mesh,
        in_specs=(
            P(None, "comp", "tile"),
            P("comp", "tile"),
            P("comp", "tile"),
            P(("comp", "tile"), None, None),
            P(("comp", "tile")),
            P(("comp", "tile"), None),
            P(("comp", "tile")),
            P(("comp", "tile")),
        ),
        out_specs=P(None, "comp", "tile"),
        check_vma=False,
    )
```

```python
import jax
import jax.numpy as jnp
from jax import lax
from jax.experimental import pallas as pl
from jax.experimental.pallas import tpu as pltpu
from jax.sharding import PartitionSpec as P

LEVELS = 60
COUPLED = 3
DEEP = LEVELS - COUPLED
BLK = 128
BY = 32
BX = 768
HALO = 4
TALL = BY + 2 * HALO
TOP = HALO + BY
SLOTS = 128
CAP = 6
PAIR = 7
TILES = 32
OCEAN = 3
BLOCKS = 192
COLS = BX // BLK
HALF = COLS // 2
WIDE = BX + BLK
KAPPA, SEA = 3, 4
LANES = 64
FIRST = 8
LAST = FIRST + HALF * BLK
LONG = LAST + 8
STRIDE = 49
WEIGHT_CHUNKS = 4
GROUP = min(16, TILES)
MESH = pl.DeviceIdType.MESH
F32 = jnp.float32
BF16 = jnp.bfloat16


def iota(shape, axis):
    return lax.broadcasted_iota(jnp.int32, shape, axis)


def split(x):
    high = x.astype(BF16)
    return high, (x - high.astype(F32)).astype(BF16)


def dot(a, b):
    return jnp.dot(a, b, preferred_element_type=F32)


def to_column(row):
    eye = iota((BLK, BLK), 0) == iota((BLK, BLK), 1)
    return jnp.sum(jnp.where(eye, row, 0.0), axis=1, keepdims=True)


def block_place(block):
    row = jnp.floor((block + 0.5) * (1.0 / COLS))
    return (block - COLS * row) * BY + row


def own(ref, *lead):
    return ref[lead + (pl.ds(HALO, BY), slice(None))]


def level_rows(slab, group, y):
    return pl.ds((slab * LANES + group * 8) * TALL + y, 8, stride=TALL)


def as_rows(ref):
    return ref.reshape(COLS * LANES * TALL, BLK)


def wide(ref, *lead):
    return jnp.concatenate([ref[lead + (j,)] for j in range(COLS + 1)], axis=1)


def neighbours(v):
    return (pltpu.roll(v, 1, 1) + pltpu.roll(v, WIDE - 1, 1)) + (
        pltpu.roll(v, 1, 0) + pltpu.roll(v, TALL - 1, 0)
    )


def step_rows(old, new, around, centre, y0, count):
    def load(ref, y, i):
        return ref[y0 + y, pl.ds(HALO + i, 8, stride=STRIDE), :]

    def one(i, carry):
        here, before = carry
        ahead = [load(old, y, i + 1) for y in range(-1, count + 1)]
        diagonal = [here[y] + ahead[y + 1] for y in range(count + 1)]
        for y in range(count):
            near = before[y] + diagonal[y]
            new[y0 + y, pl.ds(HALO + i, 8, stride=STRIDE), :] = (
                load(centre, y, i) * here[y + 1] + load(around, y, i) * near
            )
        return ahead, diagonal[1:]

    behind = [load(old, y, -1) for y in range(count)]
    here = [load(old, y, 0) for y in range(-1, count + 1)]
    before = [behind[y] + here[y + 2] for y in range(count)]
    lax.fori_loop(0, STRIDE, one, (here, before), unroll=7)


def step_blocks(old, new, around, centre, start, count, last, blocks):
    def one(b, carry):
        step_rows(old, new, around, centre, jnp.minimum(start + count * b, last), count)
        return carry

    lax.fori_loop(0, blocks, one, 0)


def step_outer(old, new, around, centre, start):
    def one(b, carry):
        step_rows(old, new, around, centre, start + b * (TOP - 2 * start), HALO)
        return carry

    lax.fori_loop(0, 2, one, 0)


def exchange_kernel(
    state, kappa, mask, weight, src, tile_of, block_of, count,
    natural, planes, sides, coef,
    field, around, centre, other, ends, weights, mask_in, small, send, received, contrib,
    load_sem, weight_sem, state_sem, remap_send, remap_recv, row_sem, side_sem,
):
    comp = lax.axis_index("comp")
    tile = lax.axis_index("tile")
    right = lax.rem(tile + 1, TILES)
    left = lax.rem(tile + TILES - 1, TILES)
    is_ocean = comp == OCEAN
    has_up = comp < OCEAN - 1
    has_down = (comp > 0) & (comp < OCEAN)

    loads = [
        pltpu.make_async_copy(part, small.at[n], load_sem.at[n])
        for n, part in enumerate((src, tile_of, block_of))
    ]
    surface_loads, kappa_loads, state_loads = [], [], []
    for j in range(COLS):
        cut = pl.ds(j * BLK, BLK)
        surface_loads.append(
            pltpu.make_async_copy(
                state.at[pl.ds(0, COUPLED), :, cut],
                planes.at[pl.ds(0, COUPLED), j, pl.ds(HALO, BY), :],
                load_sem.at[4 + j],
            )
        )
        kappa_loads.append(
            pltpu.make_async_copy(
                kappa.at[:, cut], planes.at[KAPPA, j, pl.ds(HALO, BY), :], load_sem.at[10 + j]
            )
        )
        state_loads.append(
            pltpu.make_async_copy(
                state.at[pl.ds(COUPLED, DEEP), :, cut],
                natural.at[j, pl.ds(0, DEEP), pl.ds(0, BY), :],
                state_sem.at[j],
            )
        )
    mask_load = pltpu.make_async_copy(mask, mask_in, load_sem.at[16])
    per = SLOTS // WEIGHT_CHUNKS
    weight_loads = [
        pltpu.make_async_copy(weight.at[pl.ds(n * per, per)], weights.at[pl.ds(n * per, per)], weight_sem.at[n])
        for n in range(WEIGHT_CHUNKS)
    ]
    for copy in loads + kappa_loads + [mask_load] + state_loads + surface_loads + weight_loads:
        copy.start()

    barrier = pltpu.get_barrier_semaphore()

    def greet(c, t):
        pl.semaphore_signal(barrier, inc=1, device_id=(c, t), device_id_type=MESH)

    greet(comp, left)
    greet(comp, right)

    @pl.when(has_up)
    def _():
        for t in (tile, left, right):
            greet(comp + 1, t)

    @pl.when(has_down)
    def _():
        for t in (tile, left, right):
            greet(comp - 1, t)

    @pl.when(is_ocean)
    def _():
        def body(i, carry):
            greet(i // TILES, lax.rem(i + tile, TILES))
            return carry

        lax.fori_loop(0, OCEAN * TILES, body, 0)

    @pl.when(jnp.logical_not(is_ocean))
    def _():
        def body(i, carry):
            greet(OCEAN, lax.rem(i + tile, TILES))
            return carry

        lax.fori_loop(0, TILES, body, 0)

    received[:, PAIR:, :] = jnp.zeros((received.shape[0], 8 - PAIR, received.shape[2]), F32)

    ocean_f = jnp.where(is_ocean, 1.0, 0.0)

    for copy in kappa_loads:
        copy.wait()
    mask_load.wait()
    row = iota((TALL, BLK), 0)
    beyond = ((row < HALO) & jnp.logical_not(has_down)) | ((row >= TOP) & jnp.logical_not(has_up))
    inside = jnp.where(beyond, 0.0, 1.0)
    for j in range(COLS):
        planes[SEA, j] = inside
        planes[SEA, j, pl.ds(HALO, BY), :] = jnp.maximum(
            mask_in[:, j * BLK : (j + 1) * BLK].astype(F32), 1.0 - ocean_f
        )

    sides_in = has_up.astype(jnp.int32) + has_down.astype(jnp.int32)
    pl.semaphore_wait(barrier, jnp.where(is_ocean, OCEAN * TILES + 2, TILES + 2 + 3 * sides_in))

    def remote(source, target, sems, n, device):
        return pltpu.make_async_remote_copy(
            src_ref=source,
            dst_ref=target,
            send_sem=sems.at[0, n],
            recv_sem=sems.at[1, n],
            device_id=device,
            device_id_type=MESH,
        )

    def row_copies(cut, sems, n):
        return [
            (has_up, has_down, remote(cut(TOP - HALO), cut(0), sems, n, (comp + 1, tile))),
            (has_down, has_up, remote(cut(HALO), cut(TOP), sems, n + 1, (comp - 1, tile))),
        ]

    def column_copies(source, target, sems, n):
        out = []
        for side, there in ((0, left), (1, right)):
            out += [
                (None, None, remote(source(side, HALO, BY), target(side, HALO, BY), sems, n, (comp, there))),
                (has_up, has_down, remote(
                    source(side, TOP - HALO, HALO), target(side, 0, HALO), sems, n + 1, (comp + 1, there))),
                (has_down, has_up, remote(
                    source(side, HALO, HALO), target(side, TOP, HALO), sems, n + 2, (comp - 1, there))),
            ]
            n += 3
        return out

    def each(copies, pick, act):
        for entry in copies:
            cond, copy = entry[pick], entry[2]
            if cond is None:
                act(copy)()
            else:
                pl.when(cond)(act(copy))

    def start(copies):
        each(copies, 0, lambda copy: copy.start)

    def wait_recv(copies):
        each(copies, 1, lambda copy: copy.wait_recv)

    def wait_send(copies):
        each(copies, 0, lambda copy: copy.wait_send)

    def plane_rows(first, number):
        return lambda y: planes.at[pl.ds(first, number), pl.ds(0, COLS), pl.ds(y, HALO), :]

    def plane_edge(first, number):
        return lambda side, y, rows: planes.at[pl.ds(first, number), side * (COLS - 1), pl.ds(y, rows), :]

    def side_edge(first, number):
        return lambda side, y, rows: sides.at[side, pl.ds(first, number), pl.ds(y, rows), :]

    early = row_copies(plane_rows(KAPPA, 1), row_sem, 0) + column_copies(
        plane_edge(KAPPA, 2), side_edge(KAPPA, 2), side_sem, 0
    )
    start(early)

    deep_rows = []
    for j in range(COLS):
        for up, down, base, at, there, n in (
            (has_up, has_down, BY - HALO, BY, comp + 1, 4 + j),
            (has_down, has_up, 0, TOP, comp - 1, 4 + COLS + j),
        ):
            deep_rows.append((up, down, remote(
                state.at[pl.ds(COUPLED, DEEP), pl.ds(base, HALO), pl.ds(j * BLK, BLK)],
                natural.at[j, pl.ds(0, DEEP), pl.ds(at, HALO), :],
                row_sem, n, (there, tile),
            )))
    start(deep_rows[:COLS])

    for copy in state_loads:
        copy.wait()
    flat = as_rows(natural)

    def turn(source, target):
        for j in range(HALF):
            parts = []
            for slab in (j, j + HALF):
                sea = planes[SEA, slab, pl.ds(target, 1), :] > 0.0
                for g in range(LANES // 8):
                    parts.append(jnp.where(sea, flat[level_rows(slab, g, source), :], 0.0))
            field[target, pl.ds(FIRST + j * BLK, BLK), :] = jnp.concatenate(parts, axis=0).T

    def turn_rows(source, target, number):
        def one(i, carry):
            turn(source + i, target + i)
            return carry

        lax.fori_loop(0, number, one, 0, unroll=4)

    def turn_back(y, carry):
        for j in range(HALF):
            back = field[HALO + y, pl.ds(FIRST + j * BLK, BLK), :].T
            for h, slab in enumerate((j, j + HALF)):
                sea = planes[SEA, slab, pl.ds(HALO + y, 1), :] > 0.0
                for g in range(LANES // 8):
                    at = level_rows(slab, g, y)
                    piece = back[h * LANES + g * 8 : h * LANES + g * 8 + 8]
                    flat[at, :] = jnp.where(sea, piece, flat[at, :])
        return carry

    turn_rows(0, HALO, BY)
    deep_sides = column_copies(
        lambda side, y, rows: field.at[pl.ds(y, rows), pl.ds(LAST - HALO if side else FIRST, HALO), :],
        lambda side, y, rows: ends.at[side, pl.ds(y, rows), pl.ds(HALO if side else 0, HALO), :],
        side_sem, 6,
    )
    start(deep_sides)

    start(deep_rows[COLS:])

    for copy in loads + surface_loads:
        copy.wait()
    surface = jnp.concatenate(
        [
            jnp.concatenate(
                [own(planes, f, j) for j in range(COLS)] + [jnp.zeros((64, BLK), F32)], axis=0
            )
            for f in range(COUPLED)
        ],
        axis=1,
    ).astype(BF16)
    src_place = to_column(block_place(small[0].astype(F32)))
    gather = (iota((BLK, 256), 1).astype(F32) == src_place).astype(BF16)
    picked_all = dot(gather, surface)
    active = iota((1, BLK), 1) < count[0]
    tile_row = small[1].astype(F32)
    tile_col = to_column(tile_row)
    same = tile_col == tile_row
    sub_i, lane_i = iota((BLK, BLK), 0), iota((BLK, BLK), 1)
    order_row = jnp.sum(jnp.where(same & (sub_i < lane_i), 1.0, 0.0), axis=0, keepdims=True)
    order_col = jnp.sum(jnp.where(same & (lane_i < sub_i), 1.0, 0.0), axis=1, keepdims=True)
    slot_iota = iota((TILES * 8, BLK), 0).astype(F32)
    place = (slot_iota == jnp.where(active, tile_row * 8.0 + order_row, -1.0)).astype(BF16)
    block = small[2].astype(F32)
    strip = jnp.floor((block + 0.5) * (1.0 / BLOCKS))
    code = (ocean_f * strip + (1.0 - ocean_f) * OCEAN) * BLOCKS + block_place(block - BLOCKS * strip) + 1.0
    code_high = jnp.floor(code * (1.0 / 32.0))
    code_low = code - 32.0 * code_high
    code_slot = slot_iota == jnp.where(active, tile_row * 8.0 + CAP, -1.0)
    lane_base = (lax.rem(tile, GROUP) * 8).astype(F32)
    spots = (iota((BLK, BLK), 1).astype(F32) == lane_base + order_col).astype(BF16)
    codes = 32.0 * dot(jnp.where(code_slot, code_high, 0.0).astype(BF16), spots) + dot(
        jnp.where(code_slot, code_low, 0.0).astype(BF16), spots
    )
    sub = iota((32, BLK), 0) % 8
    for n in range(WEIGHT_CHUNKS):
        weight_loads[n].wait()
        for g in range(per // 8):
            base = n * per + g * 8
            picked = picked_all[base : base + 8]
            lhs = jnp.concatenate(
                [picked[:, f * BLK : (f + 1) * BLK] for f in range(COUPLED)] + [jnp.zeros((8, BLK), F32)], axis=0
            )
            spread = jnp.concatenate([jnp.where(sub == k, lhs, 0.0) for k in range(8)], axis=1).astype(BF16)
            product = dot(spread, weights[pl.ds(base, 8)].reshape(8 * BLK, BLK))
            for f in range(COUPLED):
                contrib[pl.ds(base, 8), f * BLK : (f + 1) * BLK] = product[8 * f : 8 * f + 8]

    high, low = split(contrib[...])
    buckets = dot(place, high) + dot(place, low)
    buckets = jnp.concatenate([buckets[:, :BLK] + codes, buckets[:, BLK:]], axis=1)
    send[...] = buckets.reshape(TILES, 8, COUPLED * BLK)

    @pl.when(is_ocean)
    def _():
        def body(i, carry):
            t = lax.rem(i + tile, TILES)
            pltpu.make_async_remote_copy(
                src_ref=send.at[t, pl.ds(0, PAIR)],
                dst_ref=received.at[tile, pl.ds(0, PAIR)],
                send_sem=remap_send,
                recv_sem=remap_recv,
                device_id=(i // TILES, t),
                device_id_type=MESH,
            ).start()
            return carry

        lax.fori_loop(0, OCEAN * TILES, body, 0)

    @pl.when(jnp.logical_not(is_ocean))
    def _():
        def body(i, carry):
            t = lax.rem(i + tile, TILES)
            pltpu.make_async_remote_copy(
                src_ref=send.at[t, pl.ds(0, PAIR)],
                dst_ref=received.at[comp * TILES + tile, pl.ds(0, PAIR)],
                send_sem=remap_send,
                recv_sem=remap_recv,
                device_id=(OCEAN, t),
                device_id_type=MESH,
            ).start()
            return carry

        lax.fori_loop(0, TILES, body, 0)

    wait_recv(early)
    lane = iota((TALL, BLK), 1)
    for side in range(2):
        sides[side, SEA, pl.ds(0, HALO), :] = inside[:HALO]
        sides[side, SEA, pl.ds(TOP, HALO), :] = inside[TOP:]
    for p in (KAPPA, SEA):
        planes[p, COLS] = jnp.where(lane < BLK // 2, sides[0, p], sides[1, p])
    sea = wide(planes, SEA)
    scale = jnp.where(sea > 0.0, wide(planes, KAPPA), 0.0)
    middle = 1.0 - scale * neighbours(sea)
    for n, value in enumerate((middle, scale)):
        tiles = [value[:, j * BLK : (j + 1) * BLK] for j in range(COLS + 1)]
        for j in range(COLS + 1):
            coef[n, j] = tiles[j]
        coef[n, COLS + 1] = jnp.where(lane < BLK // 2, tiles[HALF], tiles[COLS])
        coef[n, COLS + 2] = jnp.where(lane < BLK // 2, tiles[COLS], tiles[HALF - 1])

    def spread_row(y, carry):
        for n, target in enumerate((centre, around)):
            for a, b, at in [(j, j + HALF, FIRST + j * BLK) for j in range(HALF)] + [(COLS + 1, COLS + 2, None)]:
                both = jnp.concatenate(
                    [
                        jnp.broadcast_to(coef[n, a, pl.ds(y, 1), :], (LANES, BLK)),
                        jnp.broadcast_to(coef[n, b, pl.ds(y, 1), :], (LANES, BLK)),
                    ],
                    axis=0,
                ).T
                if at is None:
                    target[y, pl.ds(LAST, 8), :] = both[:8]
                    target[y, pl.ds(0, 8), :] = both[BLK - 8 :]
                else:
                    target[y, pl.ds(at, BLK), :] = both
        return carry

    lax.fori_loop(0, TALL, spread_row, 0, unroll=2)

    def join(y, carry):
        low = iota((8, BLK), 1) < LANES
        first = field[y, pl.ds(FIRST, 8), :]
        last = field[y, pl.ds(LAST - 8, 8), :]
        field[y, pl.ds(LAST, 8), :] = pltpu.roll(jnp.where(low, ends[0, y], first), LANES, 1)
        field[y, pl.ds(0, 8), :] = pltpu.roll(jnp.where(low, last, ends[1, y]), LANES, 1)
        return carry

    wait_recv(deep_sides)
    lax.fori_loop(HALO, TOP, join, 0, unroll=4)
    step_blocks(field, other, around, centre, 5, 10, 25, 3)
    wait_send(deep_sides)
    step_blocks(other, field, around, centre, 6, 7, 27, 4)
    step_blocks(field, other, around, centre, 7, 9, 24, 3)
    step_blocks(other, field, around, centre, 8, 8, 24, 3)
    lax.fori_loop(HALO, BY - HALO, turn_back, 0, unroll=4)

    def accumulate(sources):
        whole = received.at[pl.ds(0, sources), pl.ds(0, PAIR)]
        pltpu.make_async_copy(whole, whole, remap_recv).wait()
        heads = received[pl.ds(0, sources), CAP, :BLK]
        offset = 1.0 + BLOCKS * comp.astype(F32)
        total = jnp.zeros((BLOCKS, COUPLED * BLK), F32)
        for g in range(sources // GROUP):
            codes_in = jnp.sum(heads[GROUP * g : GROUP * g + GROUP], axis=0, keepdims=True) - offset
            codes_in = codes_in[:, : GROUP * 8]
            onehot = (iota((BLOCKS, GROUP * 8), 0).astype(F32) == codes_in).astype(BF16)
            values = received[pl.ds(GROUP * g, GROUP)].reshape(GROUP * 8, COUPLED * BLK)
            big, little = split(values)
            total = total + dot(onehot, big) + dot(onehot, little)
        for j in range(COLS):
            weight_here = 0.5 * mask_in[:, j * BLK : (j + 1) * BLK].astype(F32)
            for f in range(COUPLED):
                old = own(planes, f, j)
                new = total[j * BY : (j + 1) * BY, f * BLK : (f + 1) * BLK]
                planes[f, j, pl.ds(HALO, BY), :] = old + weight_here * (new - old)

    pl.when(is_ocean)(lambda: accumulate(OCEAN * TILES))
    pl.when(jnp.logical_not(is_ocean))(lambda: accumulate(TILES))

    late = row_copies(plane_rows(0, COUPLED), row_sem, 2) + column_copies(
        plane_edge(0, COUPLED), side_edge(0, COUPLED), side_sem, 12
    )
    start(late)

    wait_recv(deep_rows)

    @pl.when(has_down)
    def _():
        turn_rows(BY, 0, HALO)
        lax.fori_loop(0, HALO, join, 0, unroll=4)

    @pl.when(has_up)
    def _():
        turn_rows(TOP, TOP, HALO)
        lax.fori_loop(TOP, TALL, join, 0, unroll=4)

    @pl.when(jnp.logical_not(has_down))
    def _():
        field[pl.ds(0, HALO)] = jnp.zeros((HALO, LONG, BLK), F32)

    @pl.when(jnp.logical_not(has_up))
    def _():
        field[pl.ds(TOP, HALO)] = jnp.zeros((HALO, LONG, BLK), F32)

    step_outer(field, other, around, centre, 1)
    step_outer(other, field, around, centre, 2)
    step_outer(field, other, around, centre, 3)
    step_outer(other, field, around, centre, 4)

    def turn_back_outer(i, carry):
        return turn_back(jnp.where(i < HALO, i, i + BY - 2 * HALO), carry)

    lax.fori_loop(0, 2 * HALO, turn_back_outer, 0, unroll=4)
    wait_recv(late)

    wait_send(early)
    wait_send(late)
    wait_send(deep_rows)

    @pl.when(is_ocean)
    def _():
        whole = received.at[:, pl.ds(0, PAIR)]
        pltpu.make_async_copy(whole, whole, remap_send).wait()

    @pl.when(jnp.logical_not(is_ocean))
    def _():
        whole = received.at[pl.ds(0, TILES), pl.ds(0, PAIR)]
        pltpu.make_async_copy(whole, whole, remap_send).wait()


def finish_kernel(natural, planes, sides, coef, out, done, sem):
    copies = [
        pltpu.make_async_copy(
            natural.at[j, pl.ds(0, DEEP), pl.ds(0, BY), :],
            out.at[pl.ds(COUPLED, DEEP), :, pl.ds(j * BLK, BLK)],
            sem.at[j],
        )
        for j in range(COLS)
    ]
    for copy in copies:
        copy.start()
    lane = iota((TALL, BLK), 1)
    sea = wide(planes, SEA) > 0.0
    middle, scale = wide(coef, 0), wide(coef, 1)
    for f in range(COUPLED):
        edge = jnp.where(lane < BLK // 2, sides[0, f], sides[1, f])
        v = jnp.concatenate([planes[f, j] for j in range(COLS)] + [edge], axis=1)
        w = jnp.where(sea, v, 0.0)
        for _ in range(4):
            w = middle * w + scale * neighbours(w)
        done[f] = jnp.where(sea, w, v)[HALO:TOP, :BX]
    copies.append(pltpu.make_async_copy(done, out.at[pl.ds(0, COUPLED)], sem.at[COLS]))
    copies[-1].start()
    for copy in copies:
        copy.wait()


def shards(state, kappa, land_mask, remap_weight, remap_src, remap_tile, remap_block, remap_count):
    vmem = pl.BlockSpec(memory_space=pltpu.VMEM)
    hbm = pl.BlockSpec(memory_space=pltpu.HBM)
    kept = (
        pltpu.VMEM((COLS, LANES, TALL, BLK), F32),
        pltpu.VMEM((5, COLS + 1, TALL, BLK), F32),
        pltpu.VMEM((2, 5, TALL, BLK), F32),
        pltpu.VMEM((2, COLS + 3, TALL, BLK), F32),
    )
    operands = (
        state, kappa, land_mask, remap_weight,
        remap_src.reshape(1, SLOTS), remap_tile.reshape(1, SLOTS),
        remap_block.reshape(1, SLOTS),
    )
    dma = pltpu.SemaphoreType.DMA
    natural, planes, sides, coef = pl.pallas_call(
        exchange_kernel,
        out_shape=kept,
        in_specs=[hbm] * 7 + [pl.BlockSpec(memory_space=pltpu.SMEM)],
        out_specs=(vmem,) * len(kept),
        scratch_shapes=[
            pltpu.VMEM((TALL, LONG, BLK), F32),
            pltpu.VMEM((TALL, LONG, BLK), F32),
            pltpu.VMEM((TALL, LONG, BLK), F32),
            pltpu.VMEM((TALL, LONG, BLK), F32),
            pltpu.VMEM((2, TALL, 8, BLK), F32),
            pltpu.VMEM((SLOTS, BLK, BLK), BF16),
            pltpu.VMEM((BY, BX), jnp.int32),
            pltpu.VMEM((3, 1, SLOTS), jnp.int32),
            pltpu.VMEM((TILES, 8, COUPLED * BLK), F32),
            pltpu.VMEM((OCEAN * TILES, 8, COUPLED * BLK), F32),
            pltpu.VMEM((SLOTS, COUPLED * BLK), F32),
            dma((17,)),
            dma((WEIGHT_CHUNKS,)),
            dma((COLS,)),
            dma,
            dma,
            dma((2, 4 + 2 * COLS)),
            dma((2, 18)),
        ],
        compiler_params=pltpu.CompilerParams(
            collective_id=0, has_side_effects=True, vmem_limit_bytes=44 << 20
        ),
        name="exchange",
    )(*(pltpu.with_memory_space_constraint(x, pltpu.HBM) for x in operands), remap_count)
    return pl.pallas_call(
        finish_kernel,
        out_shape=jax.ShapeDtypeStruct((LEVELS, BY, BX), F32),
        in_specs=[vmem] * len(kept),
        out_specs=hbm,
        scratch_shapes=[pltpu.VMEM((COUPLED, BY, BX), F32), dma((COLS + 1,))],
        compiler_params=pltpu.CompilerParams(vmem_limit_bytes=16 << 20),
        name="finish",
    )(natural, planes, sides, coef)


def solution(mesh):
    return jax.shard_map(
        shards,
        mesh=mesh,
        in_specs=(
            P(None, "comp", "tile"),
            P("comp", "tile"),
            P("comp", "tile"),
            P(("comp", "tile"), None, None),
            P(("comp", "tile")),
            P(("comp", "tile"), None),
            P(("comp", "tile")),
            P(("comp", "tile")),
        ),
        out_specs=P(None, "comp", "tile"),
        check_vma=False,
    )
```

```python
import jax
import jax.numpy as jnp
from jax import lax
from jax.experimental import pallas as pl
from jax.experimental.pallas import tpu as pltpu
from jax.sharding import PartitionSpec as P

LEVELS = 60
COUPLED = 3
DEEP = LEVELS - COUPLED
BLK = 128
BY = 32
BX = 768
HALO = 4
TALL = BY + 2 * HALO
TOP = HALO + BY
SLOTS = 128
CAP = 6
PAIR = 7
TILES = 32
OCEAN = 3
BLOCKS = 192
COLS = BX // BLK
HALF = COLS // 2
WIDE = BX + BLK
KAPPA, SEA = 3, 4
LANES = 64
FIRST = 8
LAST = FIRST + HALF * BLK
LONG = LAST + 8
STRIDE = 49
WEIGHT_CHUNKS = 4
PART = 12
SLABS = 1
GROUP = min(16, TILES)
PASSED = TILES // 2
MESH = pl.DeviceIdType.MESH
F32 = jnp.float32
BF16 = jnp.bfloat16


def iota(shape, axis):
    return lax.broadcasted_iota(jnp.int32, shape, axis)


def split(x):
    high = x.astype(BF16)
    return high, (x - high.astype(F32)).astype(BF16)


def dot(a, b):
    return jnp.dot(a, b, preferred_element_type=F32)


def to_column(row):
    eye = iota((BLK, BLK), 0) == iota((BLK, BLK), 1)
    return jnp.sum(jnp.where(eye, row, 0.0), axis=1, keepdims=True)


def block_place(block):
    row = jnp.floor((block + 0.5) * (1.0 / COLS))
    return (block - COLS * row) * BY + row


def own(ref, *lead):
    return ref[lead + (pl.ds(HALO, BY), slice(None))]


def level_rows(slab, group, y):
    return pl.ds((slab * LANES + group * 8) * TALL + y, 8, stride=TALL)


def as_rows(ref):
    return ref.reshape(COLS * LANES * TALL, BLK)


def wide(ref, *lead):
    return jnp.concatenate([ref[lead + (j,)] for j in range(COLS + 1)], axis=1)


def neighbours(v):
    return (pltpu.roll(v, 1, 1) + pltpu.roll(v, WIDE - 1, 1)) + (
        pltpu.roll(v, 1, 0) + pltpu.roll(v, TALL - 1, 0)
    )


def step_rows(old, new, around, centre, y0, count):
    faces = None if not callable(centre) else [centre(y0 + y) for y in range(count)]

    def load(ref, y, i):
        return ref[y0 + y, pl.ds(HALO + i, 8, stride=STRIDE), :]

    def one(i, carry):
        here, before = carry
        ahead = [load(old, y, i + 1) for y in range(-1, count + 1)]
        diagonal = [here[y] + ahead[y + 1] for y in range(count + 1)]
        for y in range(count):
            near = before[y] + diagonal[y]
            if faces is None:
                value = load(centre, y, i) * here[y + 1] + load(around, y, i) * near
            else:
                value = here[y + 1] + load(around, y, i) * (near - faces[y] * here[y + 1])
            new[y0 + y, pl.ds(HALO + i, 8, stride=STRIDE), :] = value
        return ahead, diagonal[1:]

    behind = [load(old, y, -1) for y in range(count)]
    here = [load(old, y, 0) for y in range(-1, count + 1)]
    before = [behind[y] + here[y + 2] for y in range(count)]
    lax.fori_loop(0, STRIDE, one, (here, before), unroll=7)


def step_blocks(old, new, around, centre, start, count, last, blocks):
    def one(b, carry):
        step_rows(old, new, around, centre, jnp.minimum(start + count * b, last), count)
        return carry

    lax.fori_loop(0, blocks, one, 0)


def step_outer(old, new, around, centre, start):
    def one(b, carry):
        step_rows(old, new, around, centre, start + b * (TOP - 2 * start), HALO)
        return carry

    lax.fori_loop(0, 2, one, 0)


def exchange_kernel(
    state, kappa, mask, weight, src, tile_of, block_of, count,
    natural, planes, sides, coef,
    field, around, centre, other, ends, weights, mask_in, small, send, received, contrib,
    load_sem, weight_sem, state_sem, remap_send, remap_recv, row_sem, side_sem,
):
    comp = lax.axis_index("comp")
    tile = lax.axis_index("tile")
    right = lax.rem(tile + 1, TILES)
    left = lax.rem(tile + TILES - 1, TILES)
    is_ocean = comp == OCEAN
    has_up = comp < OCEAN - 1
    has_down = (comp > 0) & (comp < OCEAN)

    loads = [
        pltpu.make_async_copy(part, small.at[n], load_sem.at[n])
        for n, part in enumerate((src, tile_of, block_of))
    ]
    surface_loads, kappa_loads, state_loads = [], [], []
    for j in range(COLS):
        cut = pl.ds(j * BLK, BLK)
        surface_loads.append(
            pltpu.make_async_copy(
                state.at[pl.ds(0, COUPLED), :, cut],
                planes.at[pl.ds(0, COUPLED), j, pl.ds(HALO, BY), :],
                load_sem.at[4 + j],
            )
        )
        kappa_loads.append(
            pltpu.make_async_copy(
                kappa.at[:, cut], planes.at[KAPPA, j, pl.ds(HALO, BY), :], load_sem.at[10 + j]
            )
        )
        state_loads.append(
            pltpu.make_async_copy(
                state.at[pl.ds(COUPLED, DEEP), :, cut],
                natural.at[j, pl.ds(0, DEEP), pl.ds(0, BY), :],
                state_sem.at[j],
            )
        )
    mask_load = pltpu.make_async_copy(mask, mask_in, load_sem.at[16])
    per = SLOTS // WEIGHT_CHUNKS
    weight_loads = [
        pltpu.make_async_copy(weight.at[pl.ds(n * per, per)], weights.at[pl.ds(n * per, per)], weight_sem.at[n])
        for n in range(WEIGHT_CHUNKS)
    ]
    for copy in loads + surface_loads + weight_loads + kappa_loads + [mask_load] + state_loads:
        copy.start()

    barrier = pltpu.get_barrier_semaphore()

    def greet(c, t):
        pl.semaphore_signal(barrier, inc=1, device_id=(c, t), device_id_type=MESH)

    greet(comp, left)
    greet(comp, right)

    @pl.when(has_up)
    def _():
        for t in (tile, left, right):
            greet(comp + 1, t)

    @pl.when(has_down)
    def _():
        for t in (tile, left, right):
            greet(comp - 1, t)

    @pl.when(is_ocean)
    def _():
        def body(i, carry):
            greet(i // TILES, lax.rem(i + tile, TILES))
            return carry

        lax.fori_loop(0, OCEAN * TILES, body, 0, unroll=8)

    @pl.when(jnp.logical_not(is_ocean))
    def _():
        def body(i, carry):
            greet(OCEAN, lax.rem(i + tile, TILES))
            return carry

        lax.fori_loop(0, TILES, body, 0, unroll=8)

    received[:, PAIR:, :] = jnp.zeros((received.shape[0], 8 - PAIR, received.shape[2]), F32)

    ocean_f = jnp.where(is_ocean, 1.0, 0.0)

    for copy in kappa_loads:
        copy.wait()
    mask_load.wait()
    row = iota((TALL, BLK), 0)
    beyond = ((row < HALO) & jnp.logical_not(has_down)) | ((row >= TOP) & jnp.logical_not(has_up))
    inside = jnp.where(beyond, 0.0, 1.0)
    for j in range(COLS):
        planes[SEA, j] = inside
        planes[SEA, j, pl.ds(HALO, BY), :] = jnp.maximum(
            mask_in[:, j * BLK : (j + 1) * BLK].astype(F32), 1.0 - ocean_f
        )

    for copy in loads + surface_loads:
        copy.wait()
    surface = jnp.concatenate(
        [
            jnp.concatenate(
                [own(planes, f, j) for j in range(COLS)] + [jnp.zeros((64, BLK), F32)], axis=0
            )
            for f in range(COUPLED)
        ],
        axis=1,
    ).astype(BF16)
    src_place = to_column(block_place(small[0].astype(F32)))
    gather = (iota((BLK, 256), 1).astype(F32) == src_place).astype(BF16)
    picked_all = dot(gather, surface)
    active = iota((1, BLK), 1) < count[0]
    tile_row = small[1].astype(F32)
    tile_col = to_column(tile_row)
    same = tile_col == tile_row
    sub_i, lane_i = iota((BLK, BLK), 0), iota((BLK, BLK), 1)
    order_row = jnp.sum(jnp.where(same & (sub_i < lane_i), 1.0, 0.0), axis=0, keepdims=True)
    order_col = jnp.sum(jnp.where(same & (lane_i < sub_i), 1.0, 0.0), axis=1, keepdims=True)
    slot_iota = iota((TILES * 8, BLK), 0).astype(F32)
    place = (slot_iota == jnp.where(active, tile_row * 8.0 + order_row, -1.0)).astype(BF16)
    block = small[2].astype(F32)
    strip = jnp.floor((block + 0.5) * (1.0 / BLOCKS))
    code = (ocean_f * strip + (1.0 - ocean_f) * OCEAN) * BLOCKS + block_place(block - BLOCKS * strip) + 1.0
    code_high = jnp.floor(code * (1.0 / 32.0))
    code_low = code - 32.0 * code_high
    code_slot = slot_iota == jnp.where(active, tile_row * 8.0 + CAP, -1.0)
    lane_base = (jnp.where(is_ocean, tile // 2, lax.rem(tile, GROUP)) * 8).astype(F32)
    spots = (iota((BLK, BLK), 1).astype(F32) == lane_base + order_col).astype(BF16)
    codes = 32.0 * dot(jnp.where(code_slot, code_high, 0.0).astype(BF16), spots) + dot(
        jnp.where(code_slot, code_low, 0.0).astype(BF16), spots
    )
    sub = iota((32, BLK), 0) % 8
    for n in range(WEIGHT_CHUNKS):
        weight_loads[n].wait()
        for g in range(per // 8):
            base = n * per + g * 8
            picked = picked_all[base : base + 8]
            lhs = jnp.concatenate(
                [picked[:, f * BLK : (f + 1) * BLK] for f in range(COUPLED)] + [jnp.zeros((8, BLK), F32)], axis=0
            )
            spread = jnp.concatenate([jnp.where(sub == k, lhs, 0.0) for k in range(8)], axis=1).astype(BF16)
            product = dot(spread, weights[pl.ds(base, 8)].reshape(8 * BLK, BLK))
            for f in range(COUPLED):
                contrib[pl.ds(base, 8), f * BLK : (f + 1) * BLK] = product[8 * f : 8 * f + 8]

    high, low = split(contrib[...])
    buckets = dot(place, high) + dot(place, low)
    buckets = jnp.concatenate([buckets[:, :BLK] + codes, buckets[:, BLK:]], axis=1)
    send[...] = buckets.reshape(TILES, 8, COUPLED * BLK)

    sides_in = has_up.astype(jnp.int32) + has_down.astype(jnp.int32)
    pl.semaphore_wait(barrier, jnp.where(is_ocean, OCEAN * TILES + 2, TILES + 2 + 3 * sides_in))

    def remote(source, target, sems, n, device):
        return pltpu.make_async_remote_copy(
            src_ref=source,
            dst_ref=target,
            send_sem=sems.at[0, n],
            recv_sem=sems.at[1, n],
            device_id=device,
            device_id_type=MESH,
        )

    def row_copies(cut, sems, n):
        return [
            (has_up, has_down, remote(cut(TOP - HALO), cut(0), sems, n, (comp + 1, tile))),
            (has_down, has_up, remote(cut(HALO), cut(TOP), sems, n + 1, (comp - 1, tile))),
        ]

    def column_copies(source, target, sems, n):
        out = []
        for side, there in ((0, left), (1, right)):
            out += [
                (None, None, remote(source(side, HALO, BY), target(side, HALO, BY), sems, n, (comp, there))),
                (has_up, has_down, remote(
                    source(side, TOP - HALO, HALO), target(side, 0, HALO), sems, n + 1, (comp + 1, there))),
                (has_down, has_up, remote(
                    source(side, HALO, HALO), target(side, TOP, HALO), sems, n + 2, (comp - 1, there))),
            ]
            n += 3
        return out

    def each(copies, pick, act):
        for entry in copies:
            cond, copy = entry[pick], entry[2]
            if cond is None:
                act(copy)()
            else:
                pl.when(cond)(act(copy))

    def start(copies):
        each(copies, 0, lambda copy: copy.start)

    def wait_recv(copies):
        each(copies, 1, lambda copy: copy.wait_recv)

    def wait_send(copies):
        each(copies, 0, lambda copy: copy.wait_send)

    def plane_rows(first, number):
        return lambda y: planes.at[pl.ds(first, number), pl.ds(0, COLS), pl.ds(y, HALO), :]

    def plane_edge(first, number):
        return lambda side, y, rows: planes.at[pl.ds(first, number), side * (COLS - 1), pl.ds(y, rows), :]

    def side_edge(first, number):
        return lambda side, y, rows: sides.at[side, pl.ds(first, number), pl.ds(y, rows), :]

    early = row_copies(plane_rows(KAPPA, 1), row_sem, 0) + column_copies(
        plane_edge(KAPPA, 2), side_edge(KAPPA, 2), side_sem, 0
    )
    start(early)

    def send_remap(first, last):
        @pl.when(is_ocean)
        def _():
            def body(i, carry):
                t = lax.rem((i // 2) * 5 + tile + 16, TILES)
                pltpu.make_async_remote_copy(
                    src_ref=send.at[t, pl.ds(0, PAIR)],
                    dst_ref=received.at[lax.rem(tile, 2) * PASSED + tile // 2, pl.ds(0, PAIR)],
                    send_sem=remap_send,
                    recv_sem=remap_recv,
                    device_id=(jnp.where(lax.rem(i, 2) == 0, lax.rem(tile, 2), OCEAN - 1), t),
                    device_id_type=MESH,
                ).start()
                return carry

            lax.fori_loop(2 * first, 2 * last, body, 0, unroll=8)

        @pl.when(jnp.logical_not(is_ocean))
        def _():
            def body(i, carry):
                t = lax.rem(i * 5 + tile + 16, TILES)
                pltpu.make_async_remote_copy(
                    src_ref=send.at[t, pl.ds(0, PAIR)],
                    dst_ref=received.at[comp * TILES + tile, pl.ds(0, PAIR)],
                    send_sem=remap_send,
                    recv_sem=remap_recv,
                    device_id=(OCEAN, t),
                    device_id_type=MESH,
                ).start()
                return carry

            lax.fori_loop(first, last, body, 0, unroll=8)

    deep_rows = []
    for j in range(COLS):
        for up, down, base, at, there, n in (
            (has_up, has_down, BY - HALO, BY, comp + 1, 4 + j),
            (has_down, has_up, 0, TOP, comp - 1, 4 + COLS + j),
        ):
            deep_rows.append((up, down, remote(
                state.at[pl.ds(COUPLED, DEEP), pl.ds(base, HALO), pl.ds(j * BLK, BLK)],
                natural.at[j, pl.ds(0, DEEP), pl.ds(at, HALO), :],
                row_sem, n, (there, tile),
            )))
    send_remap(0, PART)
    start(deep_rows[: 2 * SLABS])

    for copy in state_loads:
        copy.wait()
    flat = as_rows(natural)

    def turn(source, target):
        for j in range(HALF):
            parts = []
            for slab in (j, j + HALF):
                sea = planes[SEA, slab, pl.ds(target, 1), :] > 0.0
                for g in range(LANES // 8):
                    parts.append(jnp.where(sea, flat[level_rows(slab, g, source), :], 0.0))
            field[target, pl.ds(FIRST + j * BLK, BLK), :] = jnp.concatenate(parts, axis=0).T

    def turn_rows(source, target, number):
        def one(i, carry):
            turn(source + i, target + i)
            return carry

        lax.fori_loop(0, number, one, 0, unroll=4)

    def turn_back(y, carry):
        for j in range(HALF):
            back = field[HALO + y, pl.ds(FIRST + j * BLK, BLK), :].T
            for h, slab in enumerate((j, j + HALF)):
                sea = planes[SEA, slab, pl.ds(HALO + y, 1), :] > 0.0
                for g in range(LANES // 8):
                    at = level_rows(slab, g, y)
                    piece = back[h * LANES + g * 8 : h * LANES + g * 8 + 8]
                    flat[at, :] = jnp.where(sea, piece, flat[at, :])
        return carry

    turn_rows(0, HALO, BY)
    deep_sides = column_copies(
        lambda side, y, rows: field.at[pl.ds(y, rows), pl.ds(LAST - HALO if side else FIRST, HALO), :],
        lambda side, y, rows: ends.at[side, pl.ds(y, rows), pl.ds(HALO if side else 0, HALO), :],
        side_sem, 6,
    )
    start(deep_sides)

    send_remap(PART, TILES)

    wait_recv(early)
    lane = iota((TALL, BLK), 1)
    for side in range(2):
        sides[side, SEA, pl.ds(0, HALO), :] = inside[:HALO]
        sides[side, SEA, pl.ds(TOP, HALO), :] = inside[TOP:]
    for p in (KAPPA, SEA):
        planes[p, COLS] = jnp.where(lane < BLK // 2, sides[0, p], sides[1, p])
    sea = wide(planes, SEA)
    scale = jnp.where(sea > 0.0, wide(planes, KAPPA), 0.0)
    middle = 1.0 - scale * neighbours(sea)
    ends_of = []
    for n, value in enumerate((middle, scale)):
        tiles = [value[:, j * BLK : (j + 1) * BLK] for j in range(COLS + 1)]
        for j in range(COLS + 1):
            coef[n, j] = tiles[j]
        ends_of.append([
            jnp.where(lane < BLK // 2, tiles[HALF], tiles[COLS]),
            jnp.where(lane < BLK // 2, tiles[COLS], tiles[HALF - 1]),
        ])
    for h in range(2):
        inner = jnp.where(lane < BLK // 2, pltpu.roll(ends_of[1][h], 8, 1), pltpu.roll(ends_of[1][h], BLK - 8, 1))
        coef[h, COLS + 1] = jnp.where((lane < HALO) | (lane >= BLK - HALO), ends_of[0][h], inner)

    def spread(first, second, y):
        halves = [jnp.broadcast_to(coef[n, j, pl.ds(y, 1), :], (LANES, BLK)) for n, j in (first, second)]
        return jnp.concatenate(halves, axis=0).T

    def spread_rows(first, last, targets):
        def one(y, carry):
            for n, target in targets:
                for j in range(HALF):
                    target[y, pl.ds(FIRST + j * BLK, BLK), :] = spread((n, j), (n, j + HALF), y)
            both = spread((0, COLS + 1), (1, COLS + 1), y)
            for n, target in targets:
                target[y, pl.ds(LAST, 8), :] = both[8 * n : 8 * n + 8]
                target[y, pl.ds(0, 8), :] = both[BLK - 8 - 8 * n : BLK - 8 * n]
            return carry

        lax.fori_loop(first, last, one, 0, unroll=2)

    in_ocean = pl.when(is_ocean)
    in_air = pl.when(jnp.logical_not(is_ocean))
    in_ocean(lambda: spread_rows(HALO, TOP, ((0, centre), (1, around))))
    in_air(lambda: spread_rows(1, TALL - 1, ((1, around),)))

    start(deep_rows[2 * SLABS :])

    def join(y, carry):
        low = iota((8, BLK), 1) < LANES
        first = field[y, pl.ds(FIRST, 8), :]
        last = field[y, pl.ds(LAST - 8, 8), :]
        field[y, pl.ds(LAST, 8), :] = pltpu.roll(jnp.where(low, ends[0, y], first), LANES, 1)
        field[y, pl.ds(0, 8), :] = pltpu.roll(jnp.where(low, last, ends[1, y]), LANES, 1)
        return carry

    wait_recv(deep_sides)
    lax.fori_loop(HALO, TOP, join, 0, unroll=4)
    def four(y):
        return 4.0

    def faces(y):
        shut = ((comp == 0) & (y == HALO)) | ((comp == OCEAN - 1) & (y == TOP - 1))
        return jnp.where(shut, 3.0, 4.0)

    def sea_step(old, new):
        step_blocks(old, new, around, centre, HALO, 8, TOP - 8, 4)

    @in_ocean
    def _():
        for y in (HALO - 1, TOP):
            field[y] = jnp.zeros((LONG, BLK), F32)
            other[y] = jnp.zeros((LONG, BLK), F32)
        sea_step(field, other)

    @in_air
    def _():
        step_blocks(field, other, around, four, 5, 10, 25, 3)

    wait_send(deep_sides)

    @in_ocean
    def _():
        sea_step(other, field)
        sea_step(field, other)

    @in_air
    def _():
        step_blocks(other, field, around, four, 6, 7, 27, 4)

    mine = received.at[pl.ds(jnp.minimum(comp, 1) * PASSED, PASSED), pl.ds(0, PAIR)]
    passed = remote(mine, mine, side_sem, 18, (jnp.where(comp == 0, 1, 0), tile))

    @pl.when(comp < OCEAN - 1)
    def _():
        pltpu.make_async_copy(mine, mine, remap_recv).wait()
        passed.start()

    @in_air
    def _():
        step_blocks(field, other, around, four, 7, 9, 24, 3)

    def accumulate(sources):
        heads = received[pl.ds(0, sources), CAP, :BLK]
        offset = 1.0 + BLOCKS * comp.astype(F32)
        total = jnp.zeros((BLOCKS, COUPLED * BLK), F32)
        for g in range(sources // GROUP):
            codes_in = jnp.sum(heads[GROUP * g : GROUP * g + GROUP], axis=0, keepdims=True) - offset
            codes_in = codes_in[:, : GROUP * 8]
            onehot = (iota((BLOCKS, GROUP * 8), 0).astype(F32) == codes_in).astype(BF16)
            values = received[pl.ds(GROUP * g, GROUP)].reshape(GROUP * 8, COUPLED * BLK)
            big, little = split(values)
            total = total + dot(onehot, big) + dot(onehot, little)
        for j in range(COLS):
            weight_here = 0.5 * mask_in[:, j * BLK : (j + 1) * BLK].astype(F32)
            for f in range(COUPLED):
                old = own(planes, f, j)
                new = total[j * BY : (j + 1) * BY, f * BLK : (f + 1) * BLK]
                planes[f, j, pl.ds(HALO, BY), :] = old + weight_here * (new - old)

    def arrived(sources):
        whole = received.at[pl.ds(0, sources), pl.ds(0, PAIR)]
        pltpu.make_async_copy(whole, whole, remap_recv).wait()

    pl.when(comp == OCEAN - 1)(lambda: arrived(TILES))
    pl.when(comp < OCEAN - 1)(passed.wait_recv)
    in_ocean(lambda: arrived(OCEAN * TILES))
    pl.when(is_ocean)(lambda: accumulate(OCEAN * TILES))
    pl.when(jnp.logical_not(is_ocean))(lambda: accumulate(TILES))

    late = row_copies(plane_rows(0, COUPLED), row_sem, 2) + column_copies(
        plane_edge(0, COUPLED), side_edge(0, COUPLED), side_sem, 12
    )
    start(late)
    @in_ocean
    def _():
        sea_step(other, field)

    @in_air
    def _():
        step_blocks(other, field, around, four, 8, 8, 24, 3)

    lax.fori_loop(HALO, BY - HALO, turn_back, 0, unroll=4)

    wait_recv(deep_rows)

    @pl.when(has_down)
    def _():
        turn_rows(BY, 0, HALO)
        lax.fori_loop(0, HALO, join, 0, unroll=4)

    @pl.when(has_up)
    def _():
        turn_rows(TOP, TOP, HALO)
        lax.fori_loop(TOP, TALL, join, 0, unroll=4)

    @pl.when(comp == 0)
    def _():
        field[pl.ds(0, HALO)] = jnp.zeros((HALO, LONG, BLK), F32)

    @pl.when(comp == OCEAN - 1)
    def _():
        field[pl.ds(TOP, HALO)] = jnp.zeros((HALO, LONG, BLK), F32)

    @in_air
    def _():
        step_outer(field, other, around, faces, 1)
        step_outer(other, field, around, faces, 2)
        step_outer(field, other, around, faces, 3)
        step_outer(other, field, around, faces, 4)

    def turn_back_outer(i, carry):
        return turn_back(jnp.where(i < HALO, i, i + BY - 2 * HALO), carry)

    lax.fori_loop(0, 2 * HALO, turn_back_outer, 0, unroll=4)
    wait_recv(late)

    wait_send(early)
    wait_send(late)
    wait_send(deep_rows)
    pl.when(comp < OCEAN - 1)(passed.wait_send)

    @pl.when(is_ocean)
    def _():
        whole = received.at[pl.ds(0, 2 * TILES), pl.ds(0, PAIR)]
        pltpu.make_async_copy(whole, whole, remap_send).wait()

    @pl.when(jnp.logical_not(is_ocean))
    def _():
        whole = received.at[pl.ds(0, TILES), pl.ds(0, PAIR)]
        pltpu.make_async_copy(whole, whole, remap_send).wait()


def finish_kernel(natural, planes, sides, coef, out, done, sem):
    copies = [
        pltpu.make_async_copy(
            natural.at[j, pl.ds(0, DEEP), pl.ds(0, BY), :],
            out.at[pl.ds(COUPLED, DEEP), :, pl.ds(j * BLK, BLK)],
            sem.at[j],
        )
        for j in range(COLS)
    ]
    for copy in copies:
        copy.start()
    lane = iota((TALL, BLK), 1)
    sea = wide(planes, SEA) > 0.0
    middle, scale = wide(coef, 0), wide(coef, 1)
    for f in range(COUPLED):
        edge = jnp.where(lane < BLK // 2, sides[0, f], sides[1, f])
        v = jnp.concatenate([planes[f, j] for j in range(COLS)] + [edge], axis=1)
        w = jnp.where(sea, v, 0.0)
        for _ in range(4):
            w = middle * w + scale * neighbours(w)
        done[f] = jnp.where(sea, w, v)[HALO:TOP, :BX]
    copies.append(pltpu.make_async_copy(done, out.at[pl.ds(0, COUPLED)], sem.at[COLS]))
    copies[-1].start()
    for copy in copies:
        copy.wait()


def shards(state, kappa, land_mask, remap_weight, remap_src, remap_tile, remap_block, remap_count):
    vmem = pl.BlockSpec(memory_space=pltpu.VMEM)
    hbm = pl.BlockSpec(memory_space=pltpu.HBM)
    kept = (
        pltpu.VMEM((COLS, LANES, TALL, BLK), F32),
        pltpu.VMEM((5, COLS + 1, TALL, BLK), F32),
        pltpu.VMEM((2, 5, TALL, BLK), F32),
        pltpu.VMEM((2, COLS + 2, TALL, BLK), F32),
    )
    operands = (
        state, kappa, land_mask, remap_weight,
        remap_src.reshape(1, SLOTS), remap_tile.reshape(1, SLOTS),
        remap_block.reshape(1, SLOTS),
    )
    dma = pltpu.SemaphoreType.DMA
    natural, planes, sides, coef = pl.pallas_call(
        exchange_kernel,
        out_shape=kept,
        in_specs=[hbm] * 7 + [pl.BlockSpec(memory_space=pltpu.SMEM)],
        out_specs=(vmem,) * len(kept),
        scratch_shapes=[
            pltpu.VMEM((TALL, LONG, BLK), F32),
            pltpu.VMEM((TALL, LONG, BLK), F32),
            pltpu.VMEM((TALL, LONG, BLK), F32),
            pltpu.VMEM((TALL, LONG, BLK), F32),
            pltpu.VMEM((2, TALL, 8, BLK), F32),
            pltpu.VMEM((SLOTS, BLK, BLK), BF16),
            pltpu.VMEM((BY, BX), jnp.int32),
            pltpu.VMEM((3, 1, SLOTS), jnp.int32),
            pltpu.VMEM((TILES, 8, COUPLED * BLK), F32),
            pltpu.VMEM((OCEAN * TILES, 8, COUPLED * BLK), F32),
            pltpu.VMEM((SLOTS, COUPLED * BLK), F32),
            dma((17,)),
            dma((WEIGHT_CHUNKS,)),
            dma((COLS,)),
            dma,
            dma,
            dma((2, 4 + 2 * COLS)),
            dma((2, 19)),
        ],
        compiler_params=pltpu.CompilerParams(
            collective_id=0, has_side_effects=True, vmem_limit_bytes=44 << 20
        ),
        name="exchange",
    )(*(pltpu.with_memory_space_constraint(x, pltpu.HBM) for x in operands), remap_count)
    return pl.pallas_call(
        finish_kernel,
        out_shape=jax.ShapeDtypeStruct((LEVELS, BY, BX), F32),
        in_specs=[vmem] * len(kept),
        out_specs=hbm,
        scratch_shapes=[pltpu.VMEM((COUPLED, BY, BX), F32), dma((COLS + 1,))],
        compiler_params=pltpu.CompilerParams(vmem_limit_bytes=16 << 20),
        name="finish",
    )(natural, planes, sides, coef)


def solution(mesh):
    return jax.shard_map(
        shards,
        mesh=mesh,
        in_specs=(
            P(None, "comp", "tile"),
            P("comp", "tile"),
            P("comp", "tile"),
            P(("comp", "tile"), None, None),
            P(("comp", "tile")),
            P(("comp", "tile"), None),
            P(("comp", "tile")),
            P(("comp", "tile")),
        ),
        out_specs=P(None, "comp", "tile"),
        check_vma=False,
    )
```

```python
import jax
import jax.numpy as jnp
from jax import lax
from jax.experimental import pallas as pl
from jax.experimental.pallas import tpu as pltpu
from jax.sharding import PartitionSpec as P

LEVELS = 60
COUPLED = 3
DEEP = LEVELS - COUPLED
BLK = 128
BY = 32
BX = 768
HALO = 4
TALL = BY + 2 * HALO
TOP = HALO + BY
SLOTS = 128
CAP = 6
PAIR = 7
TILES = 32
OCEAN = 3
BLOCKS = 192
COLS = BX // BLK
HALF = COLS // 2
WIDE = BX + BLK
KAPPA, SEA = 3, 4
LANES = 64
FIRST = 8
LAST = FIRST + HALF * BLK
LONG = LAST + 8
STRIDE = 49
WEIGHT_CHUNKS = 4
PART = 12
SLABS = 1
GROUP = min(16, TILES)
PASSED = TILES // 2
MESH = pl.DeviceIdType.MESH
F32 = jnp.float32
BF16 = jnp.bfloat16


def iota(shape, axis):
    return lax.broadcasted_iota(jnp.int32, shape, axis)


def split(x):
    high = x.astype(BF16)
    return high, (x - high.astype(F32)).astype(BF16)


def dot(a, b):
    return jnp.dot(a, b, preferred_element_type=F32)


def to_column(row):
    eye = iota((BLK, BLK), 0) == iota((BLK, BLK), 1)
    return jnp.sum(jnp.where(eye, row, 0.0), axis=1, keepdims=True)


def block_place(block):
    row = jnp.floor((block + 0.5) * (1.0 / COLS))
    return (block - COLS * row) * BY + row


def own(ref, *lead):
    return ref[lead + (pl.ds(HALO, BY), slice(None))]


def level_rows(slab, group, y):
    return pl.ds((slab * LANES + group * 8) * TALL + y, 8, stride=TALL)


def as_rows(ref):
    return ref.reshape(COLS * LANES * TALL, BLK)


def wide(ref, *lead):
    return jnp.concatenate([ref[lead + (j,)] for j in range(COLS + 1)], axis=1)


def neighbours(v):
    return (pltpu.roll(v, 1, 1) + pltpu.roll(v, WIDE - 1, 1)) + (
        pltpu.roll(v, 1, 0) + pltpu.roll(v, TALL - 1, 0)
    )


def step_rows(old, new, around, centre, y0, count):
    faces = None if not callable(centre) else [centre(y0 + y) for y in range(count)]

    def load(ref, y, i):
        return ref[y0 + y, pl.ds(HALO + i, 8, stride=STRIDE), :]

    def one(i, carry):
        here, before = carry
        ahead = [load(old, y, i + 1) for y in range(-1, count + 1)]
        diagonal = [here[y] + ahead[y + 1] for y in range(count + 1)]
        for y in range(count):
            near = before[y] + diagonal[y]
            if faces is None:
                value = load(centre, y, i) * here[y + 1] + load(around, y, i) * near
            else:
                value = here[y + 1] + load(around, y, i) * (near - faces[y] * here[y + 1])
            new[y0 + y, pl.ds(HALO + i, 8, stride=STRIDE), :] = value
        return ahead, diagonal[1:]

    behind = [load(old, y, -1) for y in range(count)]
    here = [load(old, y, 0) for y in range(-1, count + 1)]
    before = [behind[y] + here[y + 2] for y in range(count)]
    lax.fori_loop(0, STRIDE, one, (here, before), unroll=7)


def step_blocks(old, new, around, centre, start, count, last, blocks):
    def one(b, carry):
        step_rows(old, new, around, centre, jnp.minimum(start + count * b, last), count)
        return carry

    lax.fori_loop(0, blocks, one, 0)


def step_outer(old, new, around, centre, start):
    def one(b, carry):
        step_rows(old, new, around, centre, start + b * (TOP - 2 * start), HALO)
        return carry

    lax.fori_loop(0, 2, one, 0)


def exchange_kernel(
    state, kappa, mask, weight, src, tile_of, block_of, count,
    natural, planes, sides, coef,
    field, around, centre, other, ends, weights, mask_in, small, send, received, contrib,
    load_sem, weight_sem, state_sem, remap_send, remap_recv, row_sem, side_sem,
):
    comp = lax.axis_index("comp")
    tile = lax.axis_index("tile")
    right = lax.rem(tile + 1, TILES)
    left = lax.rem(tile + TILES - 1, TILES)
    is_ocean = comp == OCEAN
    has_up = comp < OCEAN - 1
    has_down = (comp > 0) & (comp < OCEAN)

    loads = [
        pltpu.make_async_copy(part, small.at[n], load_sem.at[n])
        for n, part in enumerate((src, tile_of, block_of))
    ]
    surface_loads, kappa_loads, state_loads = [], [], []
    for j in range(COLS):
        cut = pl.ds(j * BLK, BLK)
        surface_loads.append(
            pltpu.make_async_copy(
                state.at[pl.ds(0, COUPLED), :, cut],
                planes.at[pl.ds(0, COUPLED), j, pl.ds(HALO, BY), :],
                load_sem.at[4 + j],
            )
        )
        kappa_loads.append(
            pltpu.make_async_copy(
                kappa.at[:, cut], planes.at[KAPPA, j, pl.ds(HALO, BY), :], load_sem.at[10 + j]
            )
        )
        state_loads.append(
            pltpu.make_async_copy(
                state.at[pl.ds(COUPLED, DEEP), :, cut],
                natural.at[j, pl.ds(0, DEEP), pl.ds(0, BY), :],
                state_sem.at[j],
            )
        )
    mask_load = pltpu.make_async_copy(mask, mask_in, load_sem.at[16])
    per = SLOTS // WEIGHT_CHUNKS
    weight_loads = [
        pltpu.make_async_copy(weight.at[pl.ds(n * per, per)], weights.at[pl.ds(n * per, per)], weight_sem.at[n])
        for n in range(WEIGHT_CHUNKS)
    ]
    for copy in loads + surface_loads + weight_loads + kappa_loads + [mask_load] + state_loads:
        copy.start()

    barrier = pltpu.get_barrier_semaphore()

    def greet(c, t):
        pl.semaphore_signal(barrier, inc=1, device_id=(c, t), device_id_type=MESH)

    greet(comp, left)
    greet(comp, right)

    @pl.when(has_up)
    def _():
        for t in (tile, left, right):
            greet(comp + 1, t)

    @pl.when(has_down)
    def _():
        for t in (tile, left, right):
            greet(comp - 1, t)

    @pl.when(is_ocean)
    def _():
        def body(i, carry):
            greet(i // TILES, lax.rem(i + tile, TILES))
            return carry

        lax.fori_loop(0, OCEAN * TILES, body, 0, unroll=8)

    @pl.when(jnp.logical_not(is_ocean))
    def _():
        def body(i, carry):
            greet(OCEAN, lax.rem(i + tile, TILES))
            return carry

        lax.fori_loop(0, TILES, body, 0, unroll=8)

    received[:, PAIR:, :] = jnp.zeros((received.shape[0], 8 - PAIR, received.shape[2]), F32)

    ocean_f = jnp.where(is_ocean, 1.0, 0.0)

    for copy in kappa_loads:
        copy.wait()
    mask_load.wait()
    row = iota((TALL, BLK), 0)
    beyond = ((row < HALO) & jnp.logical_not(has_down)) | ((row >= TOP) & jnp.logical_not(has_up))
    inside = jnp.where(beyond, 0.0, 1.0)
    for j in range(COLS):
        planes[SEA, j] = inside
        planes[SEA, j, pl.ds(HALO, BY), :] = jnp.maximum(
            mask_in[:, j * BLK : (j + 1) * BLK].astype(F32), 1.0 - ocean_f
        )

    for copy in loads + surface_loads:
        copy.wait()
    surface = jnp.concatenate(
        [
            jnp.concatenate(
                [own(planes, f, j) for j in range(COLS)] + [jnp.zeros((64, BLK), F32)], axis=0
            )
            for f in range(COUPLED)
        ],
        axis=1,
    ).astype(BF16)
    src_place = to_column(block_place(small[0].astype(F32)))
    gather = (iota((BLK, 256), 1).astype(F32) == src_place).astype(BF16)
    picked_all = dot(gather, surface)
    active = iota((1, BLK), 1) < count[0]
    tile_row = small[1].astype(F32)
    tile_col = to_column(tile_row)
    same = tile_col == tile_row
    sub_i, lane_i = iota((BLK, BLK), 0), iota((BLK, BLK), 1)
    order_row = jnp.sum(jnp.where(same & (sub_i < lane_i), 1.0, 0.0), axis=0, keepdims=True)
    order_col = jnp.sum(jnp.where(same & (lane_i < sub_i), 1.0, 0.0), axis=1, keepdims=True)
    slot_iota = iota((TILES * 8, BLK), 0).astype(F32)
    place = (slot_iota == jnp.where(active, tile_row * 8.0 + order_row, -1.0)).astype(BF16)
    block = small[2].astype(F32)
    strip = jnp.floor((block + 0.5) * (1.0 / BLOCKS))
    code = (ocean_f * strip + (1.0 - ocean_f) * OCEAN) * BLOCKS + block_place(block - BLOCKS * strip) + 1.0
    code_high = jnp.floor(code * (1.0 / 32.0))
    code_low = code - 32.0 * code_high
    code_slot = slot_iota == jnp.where(active, tile_row * 8.0 + CAP, -1.0)
    lane_base = (jnp.where(is_ocean, tile // 2, lax.rem(tile, GROUP)) * 8).astype(F32)
    spots = (iota((BLK, BLK), 1).astype(F32) == lane_base + order_col).astype(BF16)
    codes = 32.0 * dot(jnp.where(code_slot, code_high, 0.0).astype(BF16), spots) + dot(
        jnp.where(code_slot, code_low, 0.0).astype(BF16), spots
    )
    sub = iota((32, BLK), 0) % 8
    for n in range(WEIGHT_CHUNKS):
        weight_loads[n].wait()
        for g in range(per // 8):
            base = n * per + g * 8
            picked = picked_all[base : base + 8]
            lhs = jnp.concatenate(
                [picked[:, f * BLK : (f + 1) * BLK] for f in range(COUPLED)] + [jnp.zeros((8, BLK), F32)], axis=0
            )
            spread = jnp.concatenate([jnp.where(sub == k, lhs, 0.0) for k in range(8)], axis=1).astype(BF16)
            product = dot(spread, weights[pl.ds(base, 8)].reshape(8 * BLK, BLK))
            for f in range(COUPLED):
                contrib[pl.ds(base, 8), f * BLK : (f + 1) * BLK] = product[8 * f : 8 * f + 8]

    high, low = split(contrib[...])
    buckets = dot(place, high) + dot(place, low)
    buckets = jnp.concatenate([buckets[:, :BLK] + codes, buckets[:, BLK:]], axis=1)
    send[...] = buckets.reshape(TILES, 8, COUPLED * BLK)

    sides_in = has_up.astype(jnp.int32) + has_down.astype(jnp.int32)
    pl.semaphore_wait(barrier, jnp.where(is_ocean, OCEAN * TILES + 2, TILES + 2 + 3 * sides_in))

    def remote(source, target, sems, n, device):
        return pltpu.make_async_remote_copy(
            src_ref=source,
            dst_ref=target,
            send_sem=sems.at[0, n],
            recv_sem=sems.at[1, n],
            device_id=device,
            device_id_type=MESH,
        )

    def row_copies(cut, sems, n):
        return [
            (has_up, has_down, remote(cut(TOP - HALO), cut(0), sems, n, (comp + 1, tile))),
            (has_down, has_up, remote(cut(HALO), cut(TOP), sems, n + 1, (comp - 1, tile))),
        ]

    def column_copies(source, target, sems, n):
        out = []
        for side, there in ((0, left), (1, right)):
            out += [
                (None, None, remote(source(side, HALO, BY), target(side, HALO, BY), sems, n, (comp, there))),
                (has_up, has_down, remote(
                    source(side, TOP - HALO, HALO), target(side, 0, HALO), sems, n + 1, (comp + 1, there))),
                (has_down, has_up, remote(
                    source(side, HALO, HALO), target(side, TOP, HALO), sems, n + 2, (comp - 1, there))),
            ]
            n += 3
        return out

    def each(copies, pick, act):
        for entry in copies:
            cond, copy = entry[pick], entry[2]
            if cond is None:
                act(copy)()
            else:
                pl.when(cond)(act(copy))

    def start(copies):
        each(copies, 0, lambda copy: copy.start)

    def wait_recv(copies):
        each(copies, 1, lambda copy: copy.wait_recv)

    def wait_send(copies):
        each(copies, 0, lambda copy: copy.wait_send)

    def plane_rows(first, number):
        return lambda y: planes.at[pl.ds(first, number), pl.ds(0, COLS), pl.ds(y, HALO), :]

    def plane_edge(first, number):
        return lambda side, y, rows: planes.at[pl.ds(first, number), side * (COLS - 1), pl.ds(y, rows), :]

    def side_edge(first, number):
        return lambda side, y, rows: sides.at[side, pl.ds(first, number), pl.ds(y, rows), :]

    early = row_copies(plane_rows(KAPPA, 1), row_sem, 0) + column_copies(
        plane_edge(KAPPA, 2), side_edge(KAPPA, 2), side_sem, 0
    )
    start(early)

    def send_remap(first, last):
        @pl.when(is_ocean)
        def _():
            def body(i, carry):
                t = lax.rem((i // 2) * 5 + tile + 16, TILES)
                pltpu.make_async_remote_copy(
                    src_ref=send.at[t, pl.ds(0, PAIR)],
                    dst_ref=received.at[lax.rem(tile, 2) * PASSED + tile // 2, pl.ds(0, PAIR)],
                    send_sem=remap_send,
                    recv_sem=remap_recv,
                    device_id=(jnp.where(lax.rem(i, 2) == 0, lax.rem(tile, 2), OCEAN - 1), t),
                    device_id_type=MESH,
                ).start()
                return carry

            lax.fori_loop(2 * first, 2 * last, body, 0, unroll=8)

        @pl.when(jnp.logical_not(is_ocean))
        def _():
            def body(i, carry):
                t = lax.rem(i * 5 + tile + 16, TILES)
                pltpu.make_async_remote_copy(
                    src_ref=send.at[t, pl.ds(0, PAIR)],
                    dst_ref=received.at[comp * TILES + tile, pl.ds(0, PAIR)],
                    send_sem=remap_send,
                    recv_sem=remap_recv,
                    device_id=(OCEAN, t),
                    device_id_type=MESH,
                ).start()
                return carry

            lax.fori_loop(first, last, body, 0, unroll=8)

    deep_rows = []
    for j in range(COLS):
        for up, down, base, at, there, n in (
            (has_up, has_down, BY - HALO, BY, comp + 1, 4 + j),
            (has_down, has_up, 0, TOP, comp - 1, 4 + COLS + j),
        ):
            deep_rows.append((up, down, remote(
                state.at[pl.ds(COUPLED, DEEP), pl.ds(base, HALO), pl.ds(j * BLK, BLK)],
                natural.at[j, pl.ds(0, DEEP), pl.ds(at, HALO), :],
                row_sem, n, (there, tile),
            )))
    send_remap(0, PART)
    start(deep_rows[: 2 * SLABS])

    for copy in state_loads:
        copy.wait()
    flat = as_rows(natural)

    def turn(source, target):
        for j in range(HALF):
            parts = []
            for slab in (j, j + HALF):
                sea = planes[SEA, slab, pl.ds(target, 1), :] > 0.0
                for g in range(LANES // 8):
                    parts.append(jnp.where(sea, flat[level_rows(slab, g, source), :], 0.0))
            field[target, pl.ds(FIRST + j * BLK, BLK), :] = jnp.concatenate(parts, axis=0).T

    def turn_rows(source, target, number):
        def one(i, carry):
            turn(source + i, target + i)
            return carry

        lax.fori_loop(0, number, one, 0, unroll=4)

    def turn_back(y, carry):
        for j in range(HALF):
            back = field[HALO + y, pl.ds(FIRST + j * BLK, BLK), :].T
            for h, slab in enumerate((j, j + HALF)):
                sea = planes[SEA, slab, pl.ds(HALO + y, 1), :] > 0.0
                for g in range(LANES // 8):
                    at = level_rows(slab, g, y)
                    piece = back[h * LANES + g * 8 : h * LANES + g * 8 + 8]
                    flat[at, :] = jnp.where(sea, piece, flat[at, :])
        return carry

    turn_rows(0, HALO, BY)
    deep_sides = column_copies(
        lambda side, y, rows: field.at[pl.ds(y, rows), pl.ds(LAST - HALO if side else FIRST, HALO), :],
        lambda side, y, rows: ends.at[side, pl.ds(y, rows), pl.ds(HALO if side else 0, HALO), :],
        side_sem, 6,
    )
    start(deep_sides)

    send_remap(PART, TILES)
    start(deep_rows[2 * SLABS :])

    wait_recv(early)
    lane = iota((TALL, BLK), 1)
    for side in range(2):
        sides[side, SEA, pl.ds(0, HALO), :] = inside[:HALO]
        sides[side, SEA, pl.ds(TOP, HALO), :] = inside[TOP:]
    for p in (KAPPA, SEA):
        planes[p, COLS] = jnp.where(lane < BLK // 2, sides[0, p], sides[1, p])
    sea = wide(planes, SEA)
    scale = jnp.where(sea > 0.0, wide(planes, KAPPA), 0.0)
    middle = 1.0 - scale * neighbours(sea)
    ends_of = []
    for n, value in enumerate((middle, scale)):
        tiles = [value[:, j * BLK : (j + 1) * BLK] for j in range(COLS + 1)]
        for j in range(COLS + 1):
            coef[n, j] = tiles[j]
        ends_of.append([
            jnp.where(lane < BLK // 2, tiles[HALF], tiles[COLS]),
            jnp.where(lane < BLK // 2, tiles[COLS], tiles[HALF - 1]),
        ])
    for h in range(2):
        inner = jnp.where(lane < BLK // 2, pltpu.roll(ends_of[1][h], 8, 1), pltpu.roll(ends_of[1][h], BLK - 8, 1))
        coef[h, COLS + 1] = jnp.where((lane < HALO) | (lane >= BLK - HALO), ends_of[0][h], inner)

    def spread(first, second, y):
        halves = [jnp.broadcast_to(coef[n, j, pl.ds(y, 1), :], (LANES, BLK)) for n, j in (first, second)]
        return jnp.concatenate(halves, axis=0).T

    def spread_rows(first, last, targets):
        def one(y, carry):
            for n, target in targets:
                for j in range(HALF):
                    target[y, pl.ds(FIRST + j * BLK, BLK), :] = spread((n, j), (n, j + HALF), y)
            both = spread((0, COLS + 1), (1, COLS + 1), y)
            for n, target in targets:
                target[y, pl.ds(LAST, 8), :] = both[8 * n : 8 * n + 8]
                target[y, pl.ds(0, 8), :] = both[BLK - 8 - 8 * n : BLK - 8 * n]
            return carry

        lax.fori_loop(first, last, one, 0, unroll=2)

    in_ocean = pl.when(is_ocean)
    in_air = pl.when(jnp.logical_not(is_ocean))
    in_ocean(lambda: spread_rows(HALO, TOP, ((0, centre), (1, around))))
    in_air(lambda: spread_rows(1, TALL - 1, ((1, around),)))

    def join(y, carry):
        low = iota((8, BLK), 1) < LANES
        first = field[y, pl.ds(FIRST, 8), :]
        last = field[y, pl.ds(LAST - 8, 8), :]
        field[y, pl.ds(LAST, 8), :] = pltpu.roll(jnp.where(low, ends[0, y], first), LANES, 1)
        field[y, pl.ds(0, 8), :] = pltpu.roll(jnp.where(low, last, ends[1, y]), LANES, 1)
        return carry

    wait_recv(deep_sides)
    lax.fori_loop(HALO, TOP, join, 0, unroll=4)
    def four(y):
        return 4.0

    def faces(y):
        shut = ((comp == 0) & (y == HALO)) | ((comp == OCEAN - 1) & (y == TOP - 1))
        return jnp.where(shut, 3.0, 4.0)

    def sea_step(old, new):
        step_blocks(old, new, around, centre, HALO, 8, TOP - 8, 4)

    @in_ocean
    def _():
        for y in (HALO - 1, TOP):
            field[y] = jnp.zeros((LONG, BLK), F32)
            other[y] = jnp.zeros((LONG, BLK), F32)
        sea_step(field, other)

    @in_air
    def _():
        step_blocks(field, other, around, four, 5, 10, 25, 3)

    wait_send(deep_sides)

    @in_ocean
    def _():
        sea_step(other, field)
        sea_step(field, other)

    @in_air
    def _():
        step_blocks(other, field, around, four, 6, 7, 27, 4)

    mine = received.at[pl.ds(jnp.minimum(comp, 1) * PASSED, PASSED), pl.ds(0, PAIR)]
    passed = remote(mine, mine, side_sem, 18, (jnp.where(comp == 0, 1, 0), tile))

    @pl.when(comp < OCEAN - 1)
    def _():
        pltpu.make_async_copy(mine, mine, remap_recv).wait()
        passed.start()

    @in_air
    def _():
        step_blocks(field, other, around, four, 7, 9, 24, 3)

    def accumulate(sources):
        heads = received[pl.ds(0, sources), CAP, :BLK]
        offset = 1.0 + BLOCKS * comp.astype(F32)
        total = jnp.zeros((BLOCKS, COUPLED * BLK), F32)
        for g in range(sources // GROUP):
            codes_in = jnp.sum(heads[GROUP * g : GROUP * g + GROUP], axis=0, keepdims=True) - offset
            codes_in = codes_in[:, : GROUP * 8]
            onehot = (iota((BLOCKS, GROUP * 8), 0).astype(F32) == codes_in).astype(BF16)
            values = received[pl.ds(GROUP * g, GROUP)].reshape(GROUP * 8, COUPLED * BLK)
            big, little = split(values)
            total = total + dot(onehot, big) + dot(onehot, little)
        for j in range(COLS):
            weight_here = 0.5 * mask_in[:, j * BLK : (j + 1) * BLK].astype(F32)
            for f in range(COUPLED):
                old = own(planes, f, j)
                new = total[j * BY : (j + 1) * BY, f * BLK : (f + 1) * BLK]
                planes[f, j, pl.ds(HALO, BY), :] = old + weight_here * (new - old)

    def arrived(sources):
        whole = received.at[pl.ds(0, sources), pl.ds(0, PAIR)]
        pltpu.make_async_copy(whole, whole, remap_recv).wait()

    pl.when(comp == OCEAN - 1)(lambda: arrived(TILES))
    pl.when(comp < OCEAN - 1)(passed.wait_recv)
    in_ocean(lambda: arrived(OCEAN * TILES))
    pl.when(is_ocean)(lambda: accumulate(OCEAN * TILES))
    pl.when(jnp.logical_not(is_ocean))(lambda: accumulate(TILES))

    late = row_copies(plane_rows(0, COUPLED), row_sem, 2) + column_copies(
        plane_edge(0, COUPLED), side_edge(0, COUPLED), side_sem, 12
    )
    start(late)
    @in_ocean
    def _():
        sea_step(other, field)

    @in_air
    def _():
        step_blocks(other, field, around, four, 8, 8, 24, 3)

    lax.fori_loop(HALO, BY - HALO, turn_back, 0, unroll=4)

    wait_recv(deep_rows)

    @pl.when(has_down)
    def _():
        turn_rows(BY, 0, HALO)
        lax.fori_loop(0, HALO, join, 0, unroll=4)

    @pl.when(has_up)
    def _():
        turn_rows(TOP, TOP, HALO)
        lax.fori_loop(TOP, TALL, join, 0, unroll=4)

    @pl.when(comp == 0)
    def _():
        field[pl.ds(0, HALO)] = jnp.zeros((HALO, LONG, BLK), F32)

    @pl.when(comp == OCEAN - 1)
    def _():
        field[pl.ds(TOP, HALO)] = jnp.zeros((HALO, LONG, BLK), F32)

    @in_air
    def _():
        step_outer(field, other, around, faces, 1)
        step_outer(other, field, around, faces, 2)
        step_outer(field, other, around, faces, 3)
        step_outer(other, field, around, faces, 4)

    def turn_back_outer(i, carry):
        return turn_back(jnp.where(i < HALO, i, i + BY - 2 * HALO), carry)

    lax.fori_loop(0, 2 * HALO, turn_back_outer, 0, unroll=4)
    wait_recv(late)

    wait_send(early)
    wait_send(late)
    wait_send(deep_rows)
    pl.when(comp < OCEAN - 1)(passed.wait_send)

    @pl.when(is_ocean)
    def _():
        whole = received.at[pl.ds(0, 2 * TILES), pl.ds(0, PAIR)]
        pltpu.make_async_copy(whole, whole, remap_send).wait()

    @pl.when(jnp.logical_not(is_ocean))
    def _():
        whole = received.at[pl.ds(0, TILES), pl.ds(0, PAIR)]
        pltpu.make_async_copy(whole, whole, remap_send).wait()


def finish_kernel(natural, planes, sides, coef, out, done, sem):
    copies = [
        pltpu.make_async_copy(
            natural.at[j, pl.ds(0, DEEP), pl.ds(0, BY), :],
            out.at[pl.ds(COUPLED, DEEP), :, pl.ds(j * BLK, BLK)],
            sem.at[j],
        )
        for j in range(COLS)
    ]
    for copy in copies:
        copy.start()
    lane = iota((TALL, BLK), 1)
    sea = wide(planes, SEA) > 0.0
    middle, scale = wide(coef, 0), wide(coef, 1)
    for f in range(COUPLED):
        edge = jnp.where(lane < BLK // 2, sides[0, f], sides[1, f])
        v = jnp.concatenate([planes[f, j] for j in range(COLS)] + [edge], axis=1)
        w = jnp.where(sea, v, 0.0)
        for _ in range(4):
            w = middle * w + scale * neighbours(w)
        done[f] = jnp.where(sea, w, v)[HALO:TOP, :BX]
    copies.append(pltpu.make_async_copy(done, out.at[pl.ds(0, COUPLED)], sem.at[COLS]))
    copies[-1].start()
    for copy in copies:
        copy.wait()


def shards(state, kappa, land_mask, remap_weight, remap_src, remap_tile, remap_block, remap_count):
    vmem = pl.BlockSpec(memory_space=pltpu.VMEM)
    hbm = pl.BlockSpec(memory_space=pltpu.HBM)
    kept = (
        pltpu.VMEM((COLS, LANES, TALL, BLK), F32),
        pltpu.VMEM((5, COLS + 1, TALL, BLK), F32),
        pltpu.VMEM((2, 5, TALL, BLK), F32),
        pltpu.VMEM((2, COLS + 2, TALL, BLK), F32),
    )
    operands = (
        state, kappa, land_mask, remap_weight,
        remap_src.reshape(1, SLOTS), remap_tile.reshape(1, SLOTS),
        remap_block.reshape(1, SLOTS),
    )
    dma = pltpu.SemaphoreType.DMA
    natural, planes, sides, coef = pl.pallas_call(
        exchange_kernel,
        out_shape=kept,
        in_specs=[hbm] * 7 + [pl.BlockSpec(memory_space=pltpu.SMEM)],
        out_specs=(vmem,) * len(kept),
        scratch_shapes=[
            pltpu.VMEM((TALL, LONG, BLK), F32),
            pltpu.VMEM((TALL, LONG, BLK), F32),
            pltpu.VMEM((TALL, LONG, BLK), F32),
            pltpu.VMEM((TALL, LONG, BLK), F32),
            pltpu.VMEM((2, TALL, 8, BLK), F32),
            pltpu.VMEM((SLOTS, BLK, BLK), BF16),
            pltpu.VMEM((BY, BX), jnp.int32),
            pltpu.VMEM((3, 1, SLOTS), jnp.int32),
            pltpu.VMEM((TILES, 8, COUPLED * BLK), F32),
            pltpu.VMEM((OCEAN * TILES, 8, COUPLED * BLK), F32),
            pltpu.VMEM((SLOTS, COUPLED * BLK), F32),
            dma((17,)),
            dma((WEIGHT_CHUNKS,)),
            dma((COLS,)),
            dma,
            dma,
            dma((2, 4 + 2 * COLS)),
            dma((2, 19)),
        ],
        compiler_params=pltpu.CompilerParams(
            collective_id=0, has_side_effects=True, vmem_limit_bytes=44 << 20
        ),
        name="exchange",
    )(*(pltpu.with_memory_space_constraint(x, pltpu.HBM) for x in operands), remap_count)
    return pl.pallas_call(
        finish_kernel,
        out_shape=jax.ShapeDtypeStruct((LEVELS, BY, BX), F32),
        in_specs=[vmem] * len(kept),
        out_specs=hbm,
        scratch_shapes=[pltpu.VMEM((COUPLED, BY, BX), F32), dma((COLS + 1,))],
        compiler_params=pltpu.CompilerParams(vmem_limit_bytes=16 << 20),
        name="finish",
    )(natural, planes, sides, coef)


def solution(mesh):
    return jax.shard_map(
        shards,
        mesh=mesh,
        in_specs=(
            P(None, "comp", "tile"),
            P("comp", "tile"),
            P("comp", "tile"),
            P(("comp", "tile"), None, None),
            P(("comp", "tile")),
            P(("comp", "tile"), None),
            P(("comp", "tile")),
            P(("comp", "tile")),
        ),
        out_specs=P(None, "comp", "tile"),
        check_vma=False,
    )
```
